32 devices in a mesh: chan: 8 (over y, x, core), nbr: 4 (over z).
Axes of the slice: x: 2, y: 2, z: 4, core: 2. Of those that a mesh axis runs over, the one named last changes fastest.
Arguments:
- records: float32 [640, 28, 1280], P('chan', 'nbr'), may hold values from -112 to 112, as said below
- gap_mask: int32 [640, 28], P('chan', 'nbr'), may hold values from 0 to 1, as said below
- pair_list: int32 [8, 2, 8, 64], P('chan'), may hold values from 0 to 639, as said below
- pair_counts: int32 [8, 8], P('chan'), may hold values from 32 to 64, as said below
Outputs:
- correlations: float32 [8, 8, 64, 1024], P('chan', None, 'nbr')
The draws below stay inside these ranges and needn't reach their ends.
Inputs may be any that keep to these rules, and one draw needn't show every extreme that they name: `records`: random floats of an unknown law; no structure is promised. `gap_mask`: entries are 0 or 1; some channels are silent in every segment. `pair_list`: the source channel lies in block b, and the receiver channel is 1 to 80 channels beyond it, below 640. Slots at or beyond the live count hold pairs of the same kind that no output uses. `pair_counts`: for one owner block, every source block fills all 64 slots.
All inputs are finite; a program needn't handle non-finite values.
Results may differ from the reference program's by a relative error of at most 0.0045.
Values may be sent and summed in bfloat16 or wider, within the bound.
No kernel may reach another device: no remote copies, remote signals or barrier semaphores. Data moves between devices by JAX's collectives and lax.ppermute only.
A program may use at most 192 MiB of HBM per device.

```python
import math
import jax
import jax.numpy as jnp
from jax import lax

CH_DEV = 80
WINDOW_POINTS = 1280
NF = 256
NLAG = 1024
CAP = 64
CHANNELS = 640
SEG = 28


def draw_records(key, part):
    subkeys = jax.random.split(key, 2)
    samples = jax.random.truncated_normal(subkeys[0], -4.0, 4.0, (CHANNELS, SEG, WINDOW_POINTS), jnp.float32)
    levels = jnp.exp(jax.random.uniform(subkeys[1], (CHANNELS, SEG, 1), jnp.float32, 0.0, math.log(10.0)))
    return levels * samples


def draw_gap_mask(key, part):
    subkeys = jax.random.split(key, 2)
    silent = jax.random.randint(subkeys[0], (CHANNELS, 1), 0, 16) == 0
    levels = jax.random.randint(subkeys[1], (CHANNELS, SEG), 0, 1000)
    seg_index = jnp.arange(SEG, dtype=jnp.int32)
    thresholds = 300 + 650 * seg_index // max(SEG - 1, 1)
    usable = (levels < thresholds[None, :]).astype(jnp.int32)
    return jnp.where(silent, 0, usable).astype(jnp.int32)


def draw_pair_list(key, part):
    blocks = CHANNELS // CH_DEV
    subkeys = jax.random.split(key, 2)
    start_pos = jax.random.randint(subkeys[0], (blocks, blocks, CAP), 0, CH_DEV)
    jump_raw = jax.random.randint(subkeys[1], (blocks, blocks, CAP), 0, CH_DEV)
    block_ids = jnp.arange(blocks, dtype=jnp.int32)[:, None, None]
    owner_ids = jnp.arange(blocks, dtype=jnp.int32)[None, :, None]
    position_labels = jnp.arange(CAP, dtype=jnp.int32)[None, None, :]
    leading = (owner_ids == 0) & (position_labels == 0)
    final_block = block_ids == blocks - 1
    start_pos = jnp.where(final_block, start_pos % (CH_DEV - 1), start_pos)
    start_pos = jnp.where(leading & (block_ids == 0), 0, start_pos)
    headroom = jnp.where(final_block, CH_DEV - 1 - start_pos, CH_DEV)
    offset = 1 + jump_raw % headroom
    offset = jnp.where(leading & final_block, headroom, offset)
    anchor = block_ids * CH_DEV
    source = anchor + start_pos
    return jnp.stack([source, source + offset], axis=1).astype(jnp.int32)


def draw_pair_counts(key, part):
    blocks = CHANNELS // CH_DEV
    subkeys = jax.random.split(key, 2)
    counts = jax.random.randint(subkeys[0], (blocks, blocks), CAP // 2, CAP + 1)
    busiest = jax.random.randint(subkeys[1], (), 0, blocks)
    columns = jnp.arange(blocks, dtype=jnp.int32)[None, :]
    return jnp.where(columns == busiest, CAP, counts).astype(jnp.int32)


def setup_inputs(seed: int = 0) -> dict:
    key_list = jax.random.split(jax.random.key(seed), 5)
    records = draw_records(jax.random.fold_in(key_list[4], 71), 0)
    gap_mask = draw_gap_mask(jax.random.fold_in(key_list[4], 71), 0)
    pair_list = draw_pair_list(jax.random.fold_in(key_list[4], 71), 0)
    pair_counts = draw_pair_counts(jax.random.fold_in(key_list[4], 71), 0)
    return dict(records=records, gap_mask=gap_mask, pair_list=pair_list, pair_counts=pair_counts)


def passband_taper(bin_count):
    position = jnp.arange(bin_count, dtype=jnp.float32) + 1.0
    window = jnp.sin(math.pi * position / (bin_count + 1.0))
    return jnp.concatenate([window, window])

def inverse_table(bin_count, delay_total, window_span):
    probe_hertz = jnp.arange(bin_count, dtype=jnp.int32) + 1
    offsets = jnp.arange(delay_total, dtype=jnp.int32) - delay_total // 2
    cycle_radians = (probe_hertz[:, None] * offsets[None, :] % window_span).astype(jnp.float32) * (2.0 * math.pi / window_span)
    return jnp.concatenate([jnp.cos(cycle_radians), -jnp.sin(cycle_radians)], axis=0)

def reference(records, gap_mask, pair_list, pair_counts):
    blocks = CHANNELS // CH_DEV
    window = passband_taper(NF)

    def whiten(member):
        channel_rows, gap_flags = member
        spectrum = jnp.fft.rfft(channel_rows, axis=-1)[:, :, 1:NF + 1]
        joined = jnp.concatenate([jnp.real(spectrum), jnp.imag(spectrum)], axis=-1).astype(jnp.float32)
        energy = lax.optimization_barrier(jnp.mean(joined * joined, axis=-1, keepdims=True))
        factor = gap_flags.astype(jnp.float32)[..., None] / jnp.sqrt(energy + 1e-05)
        return (joined * factor * window).astype(jnp.bfloat16)
    whitened = lax.map(whiten, (records.reshape(blocks, CH_DEV, SEG, WINDOW_POINTS), gap_mask.reshape(blocks, CH_DEV, SEG)))
    whitened = whitened.reshape(CHANNELS, SEG, 2 * NF)
    active = gap_mask.astype(jnp.float32)
    inverse = inverse_table(NF, NLAG, WINDOW_POINTS)
    slot_index = jnp.arange(CAP, dtype=jnp.int32)

    def correlate(member):
        pair_rows, counts = member
        source = pair_rows[0].reshape(-1)
        receiver = pair_rows[1].reshape(-1)
        usable = (slot_index[None, :] < counts[:, None]).astype(jnp.float32).reshape(-1)
        source_rows = whitened[source].astype(jnp.float32)
        target_rows = whitened[receiver].astype(jnp.float32)
        source_real, source_imag = (source_rows[..., :NF], source_rows[..., NF:])
        target_real, target_imag = (target_rows[..., :NF], target_rows[..., NF:])
        cross_real = lax.optimization_barrier(jnp.sum(source_real * target_real + source_imag * target_imag, axis=1))
        cross_imag = lax.optimization_barrier(jnp.sum(source_imag * target_real - source_real * target_imag, axis=1))
        cross = jnp.concatenate([cross_real, cross_imag], axis=-1) * usable[:, None]
        intersection = lax.optimization_barrier(jnp.sum(active[source] * active[receiver], axis=1)) * usable
        stacked = cross / jnp.maximum(intersection, 1.0)[:, None]
        traces = jnp.dot(stacked, inverse, precision=lax.Precision.HIGHEST, preferred_element_type=jnp.float32)
        return traces.reshape(blocks, CAP, NLAG)
    traces = lax.map(correlate, (pair_list, pair_counts))
    return jnp.transpose(traces, (1, 0, 2, 3))
```

```python
import functools
import math

import jax
import jax.numpy as jnp
import ml_dtypes
import numpy as np
from jax import lax
from jax.experimental import pallas as pl
from jax.experimental.pallas import tpu as pltpu
from jax.sharding import PartitionSpec as P

NF = 256
NLAG = 1024
LANES = 128
BF = jnp.bfloat16
F32 = jnp.float32
VMEM = pl.BlockSpec(memory_space=pltpu.VMEM)
SMEM = pl.BlockSpec(memory_space=pltpu.SMEM)

BINS = np.concatenate([np.arange(2, NF + 1, 2), np.arange(1, NF + 1, 2)])


def two_parts(table):
    high = table.astype(ml_dtypes.bfloat16)
    return high, (table - high.astype(np.float64)).astype(ml_dtypes.bfloat16)


def forward_tables(span):
    clock = np.arange(span // 2)[:, None]
    parts = []
    for bins in (BINS[: NF // 2], BINS[NF // 2 :]):
        angle = (clock * bins[None, :] % span) * (2.0 * math.pi / span)
        parts += two_parts(np.concatenate([np.cos(angle), -np.sin(angle)], axis=1))
    return np.concatenate(parts, axis=1)


def inverse_tables(span):
    lag = np.arange(NLAG)[None, :] - NLAG // 2
    angle = (BINS[:, None] * lag % span) * (2.0 * math.pi / span)
    return two_parts(np.concatenate([np.cos(angle), -np.sin(angle)], axis=0))


def taper():
    window = np.sin(math.pi * BINS / (NF + 1.0))
    return np.concatenate([window, window])[None, :].astype(np.float32)


def halves(value):
    high = value.astype(BF)
    return high, (value - high.astype(F32)).astype(BF)


def dot(a, b):
    return jnp.dot(a, b, preferred_element_type=F32)


def as_column(row):
    size = row.shape[1]
    shape = (size, size)
    same = lax.broadcasted_iota(jnp.int32, shape, 0) == lax.broadcasted_iota(jnp.int32, shape, 1)
    return jnp.sum(jnp.where(same, row, 0.0), axis=1, keepdims=True)


def whiten_kernel(x_ref, mark_ref, table_ref, taper_ref, out_ref):
    segs, rows, span = x_ref.shape
    half, quad = span // 2, NF // 2
    flags = jnp.concatenate(
        [as_column(mark_ref[s : s + 1, :].astype(F32)) for s in range(segs)], axis=0
    )
    low = x_ref[:, :, :half].reshape(segs * rows, half)
    high = x_ref[:, :, half:].reshape(segs * rows, half)
    found = []
    for i, folded in enumerate((low + high, low - high)):
        coarse, fine = halves(folded)
        table = table_ref[:, 2 * i * NF : (2 * i + 1) * NF]
        rest = table_ref[:, (2 * i + 1) * NF : (2 * i + 2) * NF]
        found.append(dot(coarse, table) + dot(fine, table) + dot(coarse, rest))
    even, odd = found
    energy = jnp.sum(even * even + odd * odd, axis=1, keepdims=True) * (0.5 / NF)
    factor = flags / jnp.sqrt(energy + 1e-05)
    for place, part in enumerate((even[:, :quad], odd[:, :quad], even[:, quad:], odd[:, quad:])):
        columns = slice(place * quad, (place + 1) * quad)
        white = (part * factor * taper_ref[:, columns]).astype(BF)
        out_ref[:, :, columns] = white.reshape(segs, rows, quad)


def pairs_kernel(
    step, white_ref, next_ref, mark_ref, next_mark_ref, list_ref, count_ref, out_ref, source, receiver
):
    segs, rows, width = white_ref.shape
    owners, slots = list_ref.shape[2:]
    dests, _, _ = out_ref.shape
    per = owners * slots // dests
    anchor = lax.axis_index("chan") * rows
    for o in range(owners):
        live = lax.broadcasted_iota(jnp.int32, (1, slots), 1) < count_ref[0, o]
        first = jnp.where(live, list_ref[0, 0, o : o + 1, :] - anchor, -1).astype(F32)
        second = (list_ref[0, 1, o : o + 1, :] - anchor).astype(F32)
        spots = lax.broadcasted_iota(jnp.int32, (slots, rows), 1).astype(F32)
        where = slice(o * slots, (o + 1) * slots)
        source[where, :] = (spots == as_column(first)).astype(BF)
        column = as_column(second)
        receiver[0, where, :] = (spots == column).astype(BF)
        receiver[1, where, :] = (spots == column - rows).astype(BF)
    marks = mark_ref[...].astype(BF)
    next_marks = next_mark_ref[...].astype(BF)
    across = (((1,), (1,)), ((), ()))

    def body(i, carry):
        at = pl.ds(pl.multiple_of(i * step, step), step)
        src, own, nxt = source[at, :], receiver[0, at, :], receiver[1, at, :]
        real = jnp.zeros((step, NF), F32)
        imag = jnp.zeros((step, NF), F32)
        for s in range(segs):
            a = dot(src, white_ref[s])
            b = dot(own, white_ref[s]) + dot(nxt, next_ref[s])
            real += a[:, :NF] * b[:, :NF] + a[:, NF:] * b[:, NF:]
            imag += a[:, NF:] * b[:, :NF] - a[:, :NF] * b[:, NF:]
        both = lax.dot_general(src, marks, across, preferred_element_type=F32) * (
            lax.dot_general(own, marks, across, preferred_element_type=F32)
            + lax.dot_general(nxt, next_marks, across, preferred_element_type=F32)
        )
        shared = jnp.sum(both, axis=1, keepdims=True)
        to = pl.ds(i * (step // per), step // per)
        for block in range(2 * NF // LANES):
            part = (real, imag)[block // 2][:, (block % 2) * LANES : (block % 2 + 1) * LANES]
            out_ref[to, block * per : (block + 1) * per, :] = part.astype(BF).reshape(-1, per, LANES)
        shared = jnp.broadcast_to(shared, (step, LANES)).reshape(-1, per, LANES)
        tail = shared[:, :8, :]
        lane = lax.broadcasted_iota(jnp.int32, tail.shape, 2)
        for k in range(1, per // 8):
            tail = jnp.where(lane >= k * 8 * LANES // per, shared[:, 8 * k : 8 * k + 8, :], tail)
        out_ref[to, 2 * NF // LANES * per :, :] = tail.astype(BF)
        return carry

    lax.fori_loop(0, owners * slots // step, body, 0)


def lags_kernel(parts, per, x_ref, high_ref, low_ref, out_ref):
    dests, length, _ = x_ref.shape
    blocks = 2 * NF // LANES
    total = jnp.sum(x_ref[...].astype(F32).reshape(dests // parts, parts, length, LANES), axis=1)
    scale = 1.0 / jnp.maximum(total[:, blocks * per :, :], 1.0)
    scale = jnp.concatenate(
        [scale[:, :, k * 8 * LANES // per :][:, :, :1] for k in range(per // 8)], axis=1
    )
    stacked = jnp.concatenate(
        [
            (total[:, k * per : (k + 1) * per, :] * scale).reshape(-1, LANES)
            for k in range(blocks)
        ],
        axis=1,
    )
    coarse, fine = halves(stacked)
    traces = dot(coarse, high_ref[...]) + dot(fine, high_ref[...]) + dot(coarse, low_ref[...])
    out_ref[...] = traces.reshape(out_ref.shape)


def call(kernel, shape, args, specs, scratch=(), mib=24):
    return pl.pallas_call(
        kernel,
        out_shape=shape,
        in_specs=specs,
        out_specs=VMEM,
        scratch_shapes=list(scratch),
        compiler_params=pltpu.CompilerParams(vmem_limit_bytes=mib << 20),
    )(*args)


def local(records, gap_mask, pair_list, pair_counts):
    rows, segs, span = records.shape
    owners, slots = pair_list.shape[2:]
    chan, nbr = lax.axis_size("chan"), lax.axis_size("nbr")
    per = slots // nbr
    pairs = owners * slots
    back = [(i, i - 1) for i in range(1, chan)]
    marks = gap_mask.T
    white = call(
        whiten_kernel,
        jax.ShapeDtypeStruct((segs, rows, 2 * NF), BF),
        (jnp.transpose(records, (1, 0, 2)), marks, jnp.asarray(forward_tables(span)), jnp.asarray(taper())),
        [VMEM] * 4,
    )
    next_white = lax.ppermute(white, "chan", back)
    next_marks = lax.ppermute(marks, "chan", back)
    cross = call(
        functools.partial(pairs_kernel, min(256, pairs)),
        jax.ShapeDtypeStruct((chan * nbr, 2 * NF // LANES * per + 8, LANES), BF),
        (white, next_white, marks, next_marks, pair_list, pair_counts),
        [VMEM] * 5 + [SMEM],
        [pltpu.VMEM((pairs, rows), BF), pltpu.VMEM((2, pairs, rows), BF)],
    )
    arrived = lax.all_to_all(cross, ("chan", "nbr"), split_axis=0, concat_axis=0, tiled=True)
    high, low = inverse_tables(span)
    traces = call(
        functools.partial(lags_kernel, nbr, per),
        jax.ShapeDtypeStruct((chan, per, NLAG), F32),
        (arrived, jnp.asarray(high), jnp.asarray(low)),
        [VMEM] * 3,
        mib=32,
    )
    return traces[None]


def solution(mesh):
    return jax.shard_map(
        local,
        mesh=mesh,
        in_specs=(
            P("chan", "nbr", None),
            P("chan", "nbr"),
            P("chan", None, None, None),
            P("chan", None),
        ),
        out_specs=P("chan", None, "nbr", None),
        check_vma=False,
    )
```

```python
import functools
import math

import jax
import jax.numpy as jnp
import ml_dtypes
import numpy as np
from jax import lax
from jax.experimental import pallas as pl
from jax.experimental.pallas import tpu as pltpu
from jax.sharding import PartitionSpec as P

NF = 256
NLAG = 1024
LANES = 128
BF = jnp.bfloat16
F32 = jnp.float32
VMEM = pl.BlockSpec(memory_space=pltpu.VMEM)
HBM = pl.BlockSpec(memory_space=pltpu.HBM)
SMEM = pl.BlockSpec(memory_space=pltpu.SMEM)

EVEN, ODD = np.arange(2, NF + 1, 2), np.arange(1, NF + 1, 2)
FIRST = 3
STEP = 128


def two_parts(table):
    high = table.astype(ml_dtypes.bfloat16)
    return high, (table - high.astype(np.float64)).astype(ml_dtypes.bfloat16)


def forward_tables(span):
    clock = np.arange(span // 2)[:, None]
    parts = []
    for bins in (EVEN, ODD):
        angle = (clock * bins[None, :] % span) * (2.0 * math.pi / span)
        parts += two_parts(np.concatenate([np.cos(angle), -np.sin(angle)], axis=1))
    return np.stack(parts)


def inverse_tables(span):
    lag = np.arange(NLAG)[None, :] - NLAG // 2
    rows = []
    for bins in (EVEN, ODD):
        angle = (bins[:, None] * lag % span) * (2.0 * math.pi / span)
        rows += [np.cos(angle), -np.sin(angle)]
    return two_parts(np.concatenate(rows, axis=0))


def taper():
    window = np.sin(math.pi * np.concatenate([EVEN, EVEN, ODD, ODD]) / (NF + 1.0))
    return window[None, :].astype(np.float32)


def halves(value):
    high = value.astype(BF)
    return high, (value - high.astype(F32)).astype(BF)


def dot(a, b):
    return jnp.dot(a, b, preferred_element_type=F32)


def dot_across(a, b):
    return lax.dot_general(a, b, (((1,), (1,)), ((), ())), preferred_element_type=F32)


def as_column(row):
    size = row.shape[1]
    shape = (size, size)
    same = lax.broadcasted_iota(jnp.int32, shape, 0) == lax.broadcasted_iota(jnp.int32, shape, 1)
    return jnp.sum(jnp.where(same, row, 0.0), axis=1, keepdims=True)


def whiten(x_ref, flags, table_ref, taper_ref, out_ref, ready):
    segs, rows, span = x_ref.shape
    half = span // 2
    low = x_ref[:, :, :half].reshape(segs * rows, half)
    high = x_ref[:, :, half:].reshape(segs * rows, half)
    found = []
    for i, folded in enumerate((low + high, low - high)):
        coarse, fine = halves(folded)
        ready(i)
        found.append(
            dot(coarse, table_ref[2 * i]) + dot(fine, table_ref[2 * i]) + dot(coarse, table_ref[2 * i + 1])
        )
    even, odd = found
    energy = jnp.sum(even * even + odd * odd, axis=1, keepdims=True) * (0.5 / NF)
    factor = flags / jnp.sqrt(energy + 1e-05)
    for i, part in enumerate(found):
        columns = slice(i * NF, (i + 1) * NF)
        white = (part * factor * taper_ref[:, columns]).astype(BF)
        out_ref[:, :, columns] = white.reshape(segs, rows, NF)


def flag_columns(mark_ref, segs):
    return jnp.concatenate([as_column(mark_ref[s : s + 1, :].astype(F32)) for s in segs], axis=0)


def first_kernel(x_hbm, mark_hbm, table_hbm, taper_hbm, out_ref, rest_ref, mark_ref, table_ref, taper_ref, x, sem):
    count, total = x.shape[0], x_hbm.shape[0]
    copies = [
        pltpu.make_async_copy(mark_hbm, mark_ref, sem.at[0]),
        pltpu.make_async_copy(taper_hbm, taper_ref, sem.at[1]),
        pltpu.make_async_copy(x_hbm.at[pl.ds(0, count)], x, sem.at[2]),
        pltpu.make_async_copy(table_hbm.at[pl.ds(0, 2)], table_ref.at[pl.ds(0, 2)], sem.at[3]),
        pltpu.make_async_copy(table_hbm.at[pl.ds(2, 2)], table_ref.at[pl.ds(2, 2)], sem.at[4]),
        pltpu.make_async_copy(x_hbm.at[pl.ds(count, total - count)], rest_ref, sem.at[5]),
    ]
    for copy in copies:
        copy.start()
    for copy in copies[:3]:
        copy.wait()
    flags = flag_columns(mark_ref, range(count))
    whiten(x, flags, table_ref, taper_ref, out_ref, lambda i: copies[3 + i].wait())
    copies[5].wait()


def second_kernel(x_ref, mark_ref, table_ref, taper_ref, out_ref, mark_out):
    mark_out[...] = mark_ref[...]
    total = mark_ref.shape[0]
    flags = flag_columns(mark_ref, range(total - x_ref.shape[0], total))
    whiten(x_ref, flags, table_ref, taper_ref, out_ref, lambda i: None)


def add_products(real, imag, a, b):
    quad = NF // 2
    ar, ai, br, bi = a[:, :quad], a[:, quad:], b[:, :quad], b[:, quad:]
    return real + (ar * br + ai * bi), imag + (ai * br - ar * bi)


def sources_kernel(
    step, early_ref, late_ref, mark_ref, list_ref, count_ref,
    source_ref, sum_ref, next_ref, source_mark_ref, own_mark_ref, first, own,
):
    rows = early_ref.shape[1]
    owners, slots = list_ref.shape[2:]
    quad = NF // 2
    anchor = lax.axis_index("chan") * rows
    spots = lax.broadcasted_iota(jnp.int32, (slots, rows), 1).astype(F32)
    for o in range(owners):
        live = lax.broadcasted_iota(jnp.int32, (1, slots), 1) < count_ref[0, o]
        where = slice(o * slots, (o + 1) * slots)
        column = as_column(jnp.where(live, list_ref[0, 0, o : o + 1, :] - anchor, -1).astype(F32))
        first[where, :] = (spots == column).astype(BF)
        column = as_column((list_ref[0, 1, o : o + 1, :] - anchor).astype(F32))
        own[where, :] = (spots == column).astype(BF)
        next_ref[where, :] = (spots == column - rows).astype(BF)
    marks = mark_ref[...].astype(BF)

    def body(i, carry):
        at = pl.ds(pl.multiple_of(i * step, step), step)
        a_hot, b_hot = first[at, :], own[at, :]
        source_mark_ref[at, :] = dot_across(a_hot, marks)
        own_mark_ref[at, :] = dot_across(b_hot, marks)
        for h in range(2):
            columns = slice(h * NF, (h + 1) * NF)
            real = imag = jnp.zeros((step, quad), F32)
            seg = 0
            for ref in (early_ref, late_ref):
                for s in range(ref.shape[0]):
                    a = dot(a_hot, ref[s, :, columns])
                    source_ref[seg, at, columns] = a.astype(BF)
                    real, imag = add_products(real, imag, a, dot(b_hot, ref[s, :, columns]))
                    seg += 1
            sum_ref[at, h * NF : h * NF + quad] = real
            sum_ref[at, h * NF + quad : (h + 1) * NF] = imag
        return carry

    lax.fori_loop(0, owners * slots // step, body, 0)


def add_segments(at, base, white_ref, source_ref, hot, sums):
    quad = NF // 2
    result = []
    for h in range(2):
        columns = slice(h * NF, (h + 1) * NF)
        real, imag = sums[at, h * NF : h * NF + quad], sums[at, h * NF + quad : (h + 1) * NF]
        for s in range(white_ref.shape[0]):
            a = source_ref[base + s, at, columns].astype(F32)
            real, imag = add_products(real, imag, a, dot(hot, white_ref[s, :, columns]))
        result += [real, imag]
    return result


def early_kernel(step, white_ref, source_ref, next_ref, sum_ref, out_ref):
    quad = NF // 2

    def body(i, carry):
        at = pl.ds(pl.multiple_of(i * step, step), step)
        for k, part in enumerate(add_segments(at, 0, white_ref, source_ref, next_ref[at, :], sum_ref)):
            out_ref[at, k * quad : (k + 1) * quad] = part
        return carry

    lax.fori_loop(0, sum_ref.shape[0] // step, body, 0)


def late_kernel(
    step, base, white_ref, source_ref, next_ref, sum_ref, source_mark_ref, own_mark_ref, next_mark_ref, out_ref
):
    pairs = sum_ref.shape[0]
    per = pairs // out_ref.shape[0]
    next_marks = next_mark_ref[...].astype(BF)

    def body(i, carry):
        at = pl.ds(pl.multiple_of(i * step, step), step)
        to = pl.ds(i * (step // per), step // per)
        hot = next_ref[at, :]
        for k, part in enumerate(add_segments(at, base, white_ref, source_ref, hot, sum_ref)):
            out_ref[to, k * per : (k + 1) * per, :] = part.astype(BF).reshape(-1, per, LANES)
        both = source_mark_ref[at, :] * (own_mark_ref[at, :] + dot_across(hot, next_marks))
        shared = jnp.broadcast_to(jnp.sum(both, axis=1, keepdims=True), (step, LANES)).reshape(-1, per, LANES)
        tail = shared[:, :8, :]
        lane = lax.broadcasted_iota(jnp.int32, tail.shape, 2)
        for k in range(1, per // 8):
            tail = jnp.where(lane >= k * 8 * LANES // per, shared[:, 8 * k : 8 * k + 8, :], tail)
        out_ref[to, 2 * NF // LANES * per :, :] = tail.astype(BF)
        return carry

    lax.fori_loop(0, pairs // step, body, 0)


def lags_kernel(parts, per, x_ref, high_ref, low_ref, out_ref):
    dests, length, _ = x_ref.shape
    blocks = 2 * NF // LANES
    total = jnp.sum(x_ref[...].astype(F32).reshape(dests // parts, parts, length, LANES), axis=1)
    scale = 1.0 / jnp.maximum(total[:, blocks * per :, :], 1.0)
    scale = jnp.concatenate(
        [scale[:, :, k * 8 * LANES // per :][:, :, :1] for k in range(per // 8)], axis=1
    )
    stacked = jnp.concatenate(
        [
            (total[:, k * per : (k + 1) * per, :] * scale).reshape(-1, LANES)
            for k in range(blocks)
        ],
        axis=1,
    )
    coarse, fine = halves(stacked)
    traces = dot(coarse, high_ref[...]) + dot(fine, high_ref[...]) + dot(coarse, low_ref[...])
    out_ref[...] = traces.reshape(out_ref.shape)


def call(kernel, shape, args, specs, scratch=(), mib=24, cost=None):
    return pl.pallas_call(
        kernel,
        out_shape=shape,
        in_specs=specs,
        out_specs=[VMEM] * len(shape),
        scratch_shapes=list(scratch),
        compiler_params=pltpu.CompilerParams(vmem_limit_bytes=mib << 20),
        cost_estimate=cost,
    )(*args)


def local(records, gap_mask, pair_list, pair_counts):
    rows, segs, span = records.shape
    owners, slots = pair_list.shape[2:]
    chan, nbr = lax.axis_size("chan"), lax.axis_size("nbr")
    per = slots // nbr
    pairs = owners * slots
    step = min(STEP, pairs)
    width = 2 * NF
    back = [(i, i - 1) for i in range(1, chan)]
    shape = jax.ShapeDtypeStruct
    tables = jnp.asarray(forward_tables(span))
    early, rest, marks, tables, window = call(
        first_kernel,
        [
            shape((FIRST, rows, width), BF),
            shape((segs - FIRST, rows, span), F32),
            shape((segs, rows), jnp.int32),
            shape(tables.shape, BF),
            shape((1, width), F32),
        ],
        [pltpu.with_memory_space_constraint(v, pltpu.HBM) for v in (jnp.transpose(records, (1, 0, 2)), gap_mask.T, tables, jnp.asarray(taper()))],
        [HBM] * 4,
        [pltpu.VMEM((FIRST, rows, span), F32), pltpu.SemaphoreType.DMA((6,))],
    )
    next_early = lax.ppermute(early, "chan", back)
    late, marks = call(
        second_kernel,
        [shape((segs - FIRST, rows, width), BF), shape((segs, rows), jnp.int32)],
        (rest, marks, tables, window),
        [VMEM] * 4,
        cost=pl.CostEstimate(flops=1000, bytes_accessed=1000, transcendentals=0),
    )
    next_late = lax.ppermute(late, "chan", back)
    next_marks = lax.ppermute(marks, "chan", back)
    source, sums, hot, source_marks, own_marks = call(
        functools.partial(sources_kernel, step),
        [
            shape((segs, pairs, width), BF),
            shape((pairs, width), F32),
            shape((pairs, rows), BF),
            shape((pairs, segs), F32),
            shape((pairs, segs), F32),
        ],
        (early, late, marks, pair_list, pair_counts),
        [VMEM] * 4 + [SMEM],
        [pltpu.VMEM((pairs, rows), BF), pltpu.VMEM((pairs, rows), BF)],
        mib=40,
        cost=pl.CostEstimate(flops=1000, bytes_accessed=1000, transcendentals=0),
    )
    (sums,) = call(
        functools.partial(early_kernel, step),
        [shape((pairs, width), F32)],
        (next_early, source, hot, sums),
        [VMEM] * 4,
        mib=40,
    )
    (cross,) = call(
        functools.partial(late_kernel, step, FIRST),
        [shape((chan * nbr, width // LANES * per + 8, LANES), BF)],
        (next_late, source, hot, sums, source_marks, own_marks, next_marks),
        [VMEM] * 7,
        mib=40,
    )
    arrived = lax.all_to_all(cross, ("chan", "nbr"), split_axis=0, concat_axis=0, tiled=True)
    high, low = inverse_tables(span)
    (traces,) = call(
        functools.partial(lags_kernel, nbr, per),
        [shape((chan, per, NLAG), F32)],
        (arrived, jnp.asarray(high), jnp.asarray(low)),
        [VMEM] * 3,
    )
    return traces[None]


def solution(mesh):
    return jax.shard_map(
        local,
        mesh=mesh,
        in_specs=(
            P("chan", "nbr", None),
            P("chan", "nbr"),
            P("chan", None, None, None),
            P("chan", None),
        ),
        out_specs=P("chan", None, "nbr", None),
        check_vma=False,
    )
```

```python
import functools
import math

import jax
import jax.numpy as jnp
import ml_dtypes
import numpy as np
from jax import lax
from jax.experimental import pallas as pl
from jax.experimental.pallas import tpu as pltpu
from jax.sharding import PartitionSpec as P

NF = 256
NLAG = 1024
LANES = 128
BF = jnp.bfloat16
F32 = jnp.float32
VMEM = pl.BlockSpec(memory_space=pltpu.VMEM)
HBM = pl.BlockSpec(memory_space=pltpu.HBM)
SMEM = pl.BlockSpec(memory_space=pltpu.SMEM)

EVEN, ODD = np.arange(2, NF + 1, 2), np.arange(1, NF + 1, 2)
FIRST = 5
GROUP = 3
STEP = 128


def two_parts(table):
    high = table.astype(ml_dtypes.bfloat16)
    return high, (table - high.astype(np.float64)).astype(ml_dtypes.bfloat16)


def forward_tables(span):
    clock = np.arange(span // 2)[:, None]
    parts = []
    for bins in (EVEN, ODD):
        angle = (clock * bins[None, :] % span) * (2.0 * math.pi / span)
        parts += two_parts(np.concatenate([np.cos(angle), -np.sin(angle)], axis=1))
    return np.stack(parts)


def inverse_tables(span):
    lag = np.arange(NLAG)[None, :] - NLAG // 2
    rows = []
    for bins in (EVEN, ODD):
        angle = (bins[:, None] * lag % span) * (2.0 * math.pi / span)
        rows += [np.cos(angle), -np.sin(angle)]
    return two_parts(np.concatenate(rows, axis=0))


def taper():
    window = np.sin(math.pi * np.concatenate([EVEN, EVEN, ODD, ODD]) / (NF + 1.0))
    return window[None, :].astype(np.float32)


def halves(value):
    high = value.astype(BF)
    return high, (value - high.astype(F32)).astype(BF)


def dot(a, b):
    return jnp.dot(a, b, preferred_element_type=F32)


def dot_across(a, b):
    return lax.dot_general(a, b, (((1,), (1,)), ((), ())), preferred_element_type=F32)


def as_column(row):
    size = row.shape[1]
    shape = (size, size)
    same = lax.broadcasted_iota(jnp.int32, shape, 0) == lax.broadcasted_iota(jnp.int32, shape, 1)
    return jnp.sum(jnp.where(same, row, 0.0), axis=1, keepdims=True)


def whiten(x_ref, flags, table_ref, taper_ref, ready):
    segs, rows, span = x_ref.shape
    half = span // 2
    low = x_ref[:, :, :half].reshape(segs * rows, half)
    high = x_ref[:, :, half:].reshape(segs * rows, half)
    found = []
    for i, folded in enumerate((low + high, low - high)):
        coarse, fine = halves(folded)
        ready(i)
        found.append(
            dot(coarse, table_ref[2 * i]) + dot(fine, table_ref[2 * i]) + dot(coarse, table_ref[2 * i + 1])
        )
    even, odd = found
    energy = jnp.sum(even * even + odd * odd, axis=1, keepdims=True) * (0.5 / NF)
    factor = flags / jnp.sqrt(energy + 1e-05)
    return [
        (part * factor * taper_ref[:, i * NF : (i + 1) * NF]).astype(BF) for i, part in enumerate(found)
    ]


def whiten_kernel(x_hbm, mark_hbm, table_hbm, taper_hbm, early_ref, late_ref, x, mark, table, window, row, sem):
    total, rows, _ = x_hbm.shape
    early = early_ref.shape[0] // rows
    copies = [
        pltpu.make_async_copy(mark_hbm, mark, sem.at[0]),
        pltpu.make_async_copy(taper_hbm, window, sem.at[1]),
        pltpu.make_async_copy(x_hbm.at[pl.ds(0, GROUP)], x.at[pl.ds(0, GROUP)], sem.at[2]),
        pltpu.make_async_copy(table_hbm.at[pl.ds(0, 2)], table.at[pl.ds(0, 2)], sem.at[3]),
        pltpu.make_async_copy(table_hbm.at[pl.ds(2, 2)], table.at[pl.ds(2, 2)], sem.at[4]),
        pltpu.make_async_copy(
            x_hbm.at[pl.ds(GROUP, total - GROUP)], x.at[pl.ds(GROUP, total - GROUP)], sem.at[5]
        ),
    ]
    for copy in copies:
        copy.start()
    copies[0].wait()
    copies[1].wait()
    flags = [as_column(mark[s : s + 1, :].astype(F32)) for s in range(total)]
    row[...] = jnp.zeros(row.shape, F32)
    row[:total, :rows] = mark[...].astype(F32)
    early_ref[early * rows :, :] = row[...].astype(BF)
    copies[2].wait()
    for start, stop in ((0, GROUP), (GROUP, total)):
        column = jnp.concatenate(flags[start:stop], axis=0)
        if start == 0:
            ready = lambda i: copies[3 + i].wait()
        else:
            copies[5].wait()
            ready = lambda i: None
        for i, white in enumerate(whiten(x.at[start:stop], column, table, window, ready)):
            columns = slice(i * NF, (i + 1) * NF)
            split = min(max(early - start, 0), stop - start) * rows
            if split:
                early_ref[start * rows : start * rows + split, columns] = white[:split]
            if split < white.shape[0]:
                base = max(start - early, 0) * rows
                late_ref[base : base + white.shape[0] - split, columns] = white[split:]


def add_products(real, imag, a, b):
    quad = NF // 2
    ar, ai, br, bi = a[:, :quad], a[:, quad:], b[:, :quad], b[:, quad:]
    return real + (ar * br + ai * bi), imag + (ai * br - ar * bi)


def sources_kernel(
    step, early_ref, late_ref, mark_ref, list_ref, count_ref,
    source_ref, sum_ref, next_ref, source_mark_ref, own_mark_ref, first, own,
):
    segs, rows = mark_ref.shape
    owners, slots = list_ref.shape[2:]
    quad = NF // 2
    anchor = lax.axis_index("chan") * rows
    spots = lax.broadcasted_iota(jnp.int32, (slots, rows), 1).astype(F32)
    for o in range(owners):
        live = lax.broadcasted_iota(jnp.int32, (1, slots), 1) < count_ref[0, o]
        where = slice(o * slots, (o + 1) * slots)
        column = as_column(jnp.where(live, list_ref[0, 0, o : o + 1, :] - anchor, -1).astype(F32))
        first[where, :] = (spots == column).astype(BF)
        column = as_column((list_ref[0, 1, o : o + 1, :] - anchor).astype(F32))
        own[where, :] = (spots == column).astype(BF)
        next_ref[where, :] = (spots == column - rows).astype(BF)
    marks = mark_ref[...].astype(BF)

    def body(i, carry):
        at = pl.ds(pl.multiple_of(i * step, step), step)
        a_hot, b_hot = first[at, :], own[at, :]
        source_mark_ref[at, :] = dot_across(a_hot, marks)
        own_mark_ref[at, :] = dot_across(b_hot, marks)
        for h in range(2):
            columns = slice(h * NF, (h + 1) * NF)
            real = imag = jnp.zeros((step, quad), F32)
            for s in range(segs):
                ref, base = (early_ref, s) if s < FIRST else (late_ref, s - FIRST)
                white = ref[base * rows : (base + 1) * rows, columns]
                a = dot(a_hot, white)
                source_ref[s, at, columns] = a.astype(BF)
                real, imag = add_products(real, imag, a, dot(b_hot, white))
            sum_ref[at, h * NF : h * NF + quad] = real
            sum_ref[at, h * NF + quad : (h + 1) * NF] = imag
        return carry

    lax.fori_loop(0, owners * slots // step, body, 0)


def add_segments(at, segs, base, white_ref, source_ref, hot, sums):
    quad = NF // 2
    rows = hot.shape[1]
    result = []
    for h in range(2):
        columns = slice(h * NF, (h + 1) * NF)
        real, imag = sums[at, h * NF : h * NF + quad], sums[at, h * NF + quad : (h + 1) * NF]
        for s in range(segs):
            a = source_ref[base + s, at, columns].astype(F32)
            real, imag = add_products(real, imag, a, dot(hot, white_ref[s * rows : (s + 1) * rows, columns]))
        result += [real, imag]
    return result


def early_kernel(
    step, white_ref, source_ref, next_ref, sum_ref, source_mark_ref, own_mark_ref, out_ref, tail_ref
):
    pairs, rows = next_ref.shape
    segs = source_mark_ref.shape[1]
    per = pairs // tail_ref.shape[0]
    quad = NF // 2
    next_marks = white_ref[FIRST * rows :, :LANES].astype(F32)[:segs, :rows].astype(BF)

    def body(i, carry):
        at = pl.ds(pl.multiple_of(i * step, step), step)
        to = pl.ds(i * (step // per), step // per)
        hot = next_ref[at, :]
        for k, part in enumerate(add_segments(at, FIRST, 0, white_ref, source_ref, hot, sum_ref)):
            out_ref[at, k * quad : (k + 1) * quad] = part
        both = source_mark_ref[at, :] * (own_mark_ref[at, :] + dot_across(hot, next_marks))
        shared = jnp.broadcast_to(jnp.sum(both, axis=1, keepdims=True), (step, LANES)).reshape(-1, per, LANES)
        tail = shared[:, :8, :]
        lane = lax.broadcasted_iota(jnp.int32, tail.shape, 2)
        for k in range(1, per // 8):
            tail = jnp.where(lane >= k * 8 * LANES // per, shared[:, 8 * k : 8 * k + 8, :], tail)
        tail_ref[to, :, :] = tail
        return carry

    lax.fori_loop(0, pairs // step, body, 0)


def late_kernel(step, white_ref, source_ref, next_ref, sum_ref, tail_ref, out_ref):
    pairs = sum_ref.shape[0]
    per = pairs // out_ref.shape[0]
    late = source_ref.shape[0] - FIRST
    out_ref[:, 2 * NF // LANES * per :, :] = tail_ref[...].astype(BF)

    def body(i, carry):
        at = pl.ds(pl.multiple_of(i * step, step), step)
        to = pl.ds(i * (step // per), step // per)
        for k, part in enumerate(
            add_segments(at, late, FIRST, white_ref, source_ref, next_ref[at, :], sum_ref)
        ):
            out_ref[to, k * per : (k + 1) * per, :] = part.astype(BF).reshape(-1, per, LANES)
        return carry

    lax.fori_loop(0, pairs // step, body, 0)


def lags_kernel(parts, per, x_ref, high_ref, low_ref, out_ref):
    dests, length, _ = x_ref.shape
    blocks = 2 * NF // LANES
    total = jnp.sum(x_ref[...].astype(F32).reshape(dests // parts, parts, length, LANES), axis=1)
    scale = 1.0 / jnp.maximum(total[:, blocks * per :, :], 1.0)
    scale = jnp.concatenate(
        [scale[:, :, k * 8 * LANES // per :][:, :, :1] for k in range(per // 8)], axis=1
    )
    stacked = jnp.concatenate(
        [
            (total[:, k * per : (k + 1) * per, :] * scale).reshape(-1, LANES)
            for k in range(blocks)
        ],
        axis=1,
    )
    coarse, fine = halves(stacked)
    traces = dot(coarse, high_ref[...]) + dot(fine, high_ref[...]) + dot(coarse, low_ref[...])
    out_ref[...] = traces.reshape(out_ref.shape)


def call(kernel, shape, args, specs, scratch=(), mib=24):
    return pl.pallas_call(
        kernel,
        out_shape=shape,
        in_specs=specs,
        out_specs=[VMEM] * len(shape),
        scratch_shapes=list(scratch),
        compiler_params=pltpu.CompilerParams(vmem_limit_bytes=mib << 20),
    )(*args)


def local(records, gap_mask, pair_list, pair_counts):
    rows, segs, span = records.shape
    owners, slots = pair_list.shape[2:]
    chan, nbr = lax.axis_size("chan"), lax.axis_size("nbr")
    per = slots // nbr
    pairs = owners * slots
    step = min(STEP, pairs)
    width = 2 * NF
    back = [(i, i - 1) for i in range(1, chan)]
    shape = jax.ShapeDtypeStruct
    tables = forward_tables(span)
    inputs = (jnp.transpose(records, (1, 0, 2)), gap_mask.T, jnp.asarray(tables), jnp.asarray(taper()))
    extra = -(-segs // 16) * 16
    early, late = call(
        whiten_kernel,
        [shape((FIRST * rows + extra, width), BF), shape(((segs - FIRST) * rows, width), BF)],
        [pltpu.with_memory_space_constraint(v, pltpu.HBM) for v in inputs],
        [HBM] * 4,
        [
            pltpu.VMEM((segs, rows, span), F32),
            pltpu.VMEM((segs, rows), jnp.int32),
            pltpu.VMEM(tables.shape, BF),
            pltpu.VMEM((1, width), F32),
            pltpu.VMEM((extra, width), F32),
            pltpu.SemaphoreType.DMA((6,)),
        ],
        mib=32,
    )
    next_early = lax.ppermute(early, "chan", back)
    next_late = lax.ppermute(late, "chan", back)
    source, sums, hot, source_marks, own_marks = call(
        functools.partial(sources_kernel, step),
        [
            shape((segs, pairs, width), BF),
            shape((pairs, width), F32),
            shape((pairs, rows), BF),
            shape((pairs, segs), F32),
            shape((pairs, segs), F32),
        ],
        (early, late, gap_mask.T, pair_list, pair_counts),
        [VMEM] * 4 + [SMEM],
        [pltpu.VMEM((pairs, rows), BF), pltpu.VMEM((pairs, rows), BF)],
        mib=40,
    )
    sums, tail = call(
        functools.partial(early_kernel, step),
        [shape((pairs, width), F32), shape((chan * nbr, 8, LANES), F32)],
        (next_early, source, hot, sums, source_marks, own_marks),
        [VMEM] * 6,
        mib=40,
    )
    (cross,) = call(
        functools.partial(late_kernel, step),
        [shape((chan * nbr, width // LANES * per + 8, LANES), BF)],
        (next_late, source, hot, sums, tail),
        [VMEM] * 5,
        mib=40,
    )
    arrived = lax.all_to_all(cross, ("chan", "nbr"), split_axis=0, concat_axis=0, tiled=True)
    high, low = inverse_tables(span)
    (traces,) = call(
        functools.partial(lags_kernel, nbr, per),
        [shape((chan, per, NLAG), F32)],
        (arrived, jnp.asarray(high), jnp.asarray(low)),
        [VMEM] * 3,
    )
    return traces[None]


def solution(mesh):
    return jax.shard_map(
        local,
        mesh=mesh,
        in_specs=(
            P("chan", "nbr", None),
            P("chan", "nbr"),
            P("chan", None, None, None),
            P("chan", None),
        ),
        out_specs=P("chan", None, "nbr", None),
        check_vma=False,
    )
```

```python
import functools
import math

import jax
import jax.numpy as jnp
import ml_dtypes
import numpy as np
from jax import lax
from jax.experimental import pallas as pl
from jax.experimental.pallas import tpu as pltpu
from jax.sharding import PartitionSpec as P

NF = 256
NLAG = 1024
LANES = 128
BF = jnp.bfloat16
F32 = jnp.float32
VMEM = pl.BlockSpec(memory_space=pltpu.VMEM)
HBM = pl.BlockSpec(memory_space=pltpu.HBM)
SMEM = pl.BlockSpec(memory_space=pltpu.SMEM)

EVEN, ODD = np.arange(2, NF + 1, 2), np.arange(1, NF + 1, 2)
FIRST = 5
GROUP = 3
STEP = 512


def two_parts(table):
    high = table.astype(ml_dtypes.bfloat16)
    return high, (table - high.astype(np.float64)).astype(ml_dtypes.bfloat16)


def forward_tables(span):
    clock = np.arange(span // 2)[:, None]
    parts = []
    for bins in (EVEN, ODD):
        angle = (clock * bins[None, :] % span) * (2.0 * math.pi / span)
        table = np.concatenate([np.cos(angle), -np.sin(angle)], axis=1)
        parts.append(np.concatenate(two_parts(table), axis=0))
    return np.stack(parts)


def inverse_tables(span):
    lag = np.arange(NLAG)[None, :] - NLAG // 2
    rows = []
    for bins in (EVEN, ODD):
        angle = (bins[:, None] * lag % span) * (2.0 * math.pi / span)
        rows += [np.cos(angle), -np.sin(angle)]
    return two_parts(np.concatenate(rows, axis=0))


def taper():
    window = np.sin(math.pi * np.concatenate([EVEN, EVEN, ODD, ODD]) / (NF + 1.0))
    return window[None, :].astype(np.float32)


def halves(value):
    high = value.astype(BF)
    return high, (value - high.astype(F32)).astype(BF)


def dot(a, b):
    return jnp.dot(a, b, preferred_element_type=F32)


def dot_across(a, b):
    return lax.dot_general(a, b, (((1,), (1,)), ((), ())), preferred_element_type=F32)


def as_column(row):
    size = row.shape[1]
    shape = (size, size)
    same = lax.broadcasted_iota(jnp.int32, shape, 0) == lax.broadcasted_iota(jnp.int32, shape, 1)
    return jnp.sum(jnp.where(same, row, 0.0), axis=1, keepdims=True)


def whiten(x_ref, flags, table_ref, taper_ref):
    segs, rows, span = x_ref.shape
    half = span // 2
    low = x_ref[:, :, :half].reshape(segs * rows, half)
    high = x_ref[:, :, half:].reshape(segs * rows, half)
    found = []
    for i, folded in enumerate((low + high, low - high)):
        coarse, fine = halves(folded)
        found.append(
            dot(fine, table_ref[i, :half, :]) + dot(jnp.concatenate([coarse, coarse], axis=1), table_ref[i])
        )
    even, odd = found
    energy = jnp.sum(even * even + odd * odd, axis=1, keepdims=True) * (0.5 / NF)
    factor = flags / jnp.sqrt(energy + 1e-05)
    return [
        (part * factor * taper_ref[:, i * NF : (i + 1) * NF]).astype(BF) for i, part in enumerate(found)
    ]


def whiten_kernel(x_hbm, mark_hbm, table_hbm, taper_hbm, early_ref, late_ref, x, mark, table, window, row, sem):
    total, rows, _ = x_hbm.shape
    early = early_ref.shape[0] // rows
    small = [
        pltpu.make_async_copy(mark_hbm, mark, sem.at[0]),
        pltpu.make_async_copy(taper_hbm, window, sem.at[1]),
    ]
    tables = pltpu.make_async_copy(table_hbm, table, sem.at[2])
    groups = [
        pltpu.make_async_copy(x_hbm.at[pl.ds(a, b - a)], x.at[pl.ds(a, b - a)], sem.at[3 + i])
        for i, (a, b) in enumerate(((0, GROUP), (GROUP, total)))
    ]
    for copy in small + [tables] + groups:
        copy.start()
    for copy in small:
        copy.wait()
    flags = [as_column(mark[s : s + 1, :].astype(F32)) for s in range(total)]
    row[...] = jnp.zeros(row.shape, F32)
    row[:total, :rows] = mark[...].astype(F32)
    early_ref[early * rows :, :] = row[...].astype(BF)
    tables.wait()
    for group, (start, stop) in zip(groups, ((0, GROUP), (GROUP, total))):
        group.wait()
        column = jnp.concatenate(flags[start:stop], axis=0)
        for i, white in enumerate(whiten(x.at[start:stop], column, table, window)):
            columns = slice(i * NF, (i + 1) * NF)
            split = min(max(early - start, 0), stop - start) * rows
            if split:
                early_ref[start * rows : start * rows + split, columns] = white[:split]
            if split < white.shape[0]:
                base = max(start - early, 0) * rows
                late_ref[base : base + white.shape[0] - split, columns] = white[split:]


def add_products(real, imag, a, b):
    quad = NF // 2
    ar, ai, br, bi = a[:, :quad], a[:, quad:], b[:, :quad], b[:, quad:]
    return real + (ar * br + ai * bi), imag + (ai * br - ar * bi)


def sources_kernel(
    step, early_ref, late_ref, mark_ref, list_ref, count_ref,
    source_ref, sum_ref, next_ref, source_mark_ref, own_mark_ref, first, own,
):
    segs, rows = mark_ref.shape
    owners, slots = list_ref.shape[2:]
    quad = NF // 2
    anchor = lax.axis_index("chan") * rows
    spots = lax.broadcasted_iota(jnp.int32, (slots, rows), 1).astype(F32)
    for o in range(owners):
        live = lax.broadcasted_iota(jnp.int32, (1, slots), 1) < count_ref[0, o]
        where = slice(o * slots, (o + 1) * slots)
        column = as_column(jnp.where(live, list_ref[0, 0, o : o + 1, :] - anchor, -1).astype(F32))
        first[where, :] = (spots == column).astype(BF)
        column = as_column((list_ref[0, 1, o : o + 1, :] - anchor).astype(F32))
        own[where, :] = (spots == column).astype(BF)
        next_ref[where, :] = (spots == column - rows).astype(BF)
    marks = mark_ref[...].astype(BF)

    def body(i, carry):
        at = pl.ds(pl.multiple_of(i * step, step), step)
        a_hot, b_hot = first[at, :], own[at, :]
        source_mark_ref[at, :] = dot_across(a_hot, marks)
        own_mark_ref[at, :] = dot_across(b_hot, marks)
        for h in range(2):
            columns = slice(h * NF, (h + 1) * NF)
            real = imag = jnp.zeros((step, quad), F32)
            for s in range(segs):
                ref, base = (early_ref, s) if s < FIRST else (late_ref, s - FIRST)
                white = ref[base * rows : (base + 1) * rows, columns]
                a = dot(a_hot, white)
                source_ref[s, at, columns] = a.astype(BF)
                real, imag = add_products(real, imag, a, dot(b_hot, white))
            sum_ref[at, h * NF : h * NF + quad] = real
            sum_ref[at, h * NF + quad : (h + 1) * NF] = imag
        return carry

    lax.fori_loop(0, owners * slots // step, body, 0)


def add_segments(at, segs, base, white_ref, source_ref, hot, sums):
    quad = NF // 2
    rows = hot.shape[1]
    result = []
    for h in range(2):
        columns = slice(h * NF, (h + 1) * NF)
        real, imag = sums[at, h * NF : h * NF + quad], sums[at, h * NF + quad : (h + 1) * NF]
        for s in range(segs):
            a = source_ref[base + s, at, columns].astype(F32)
            real, imag = add_products(real, imag, a, dot(hot, white_ref[s * rows : (s + 1) * rows, columns]))
        result += [real, imag]
    return result


def early_kernel(
    step, white_ref, source_ref, next_ref, sum_ref, source_mark_ref, own_mark_ref, out_ref, tail_ref
):
    pairs, rows = next_ref.shape
    segs = source_mark_ref.shape[1]
    per = pairs // tail_ref.shape[0]
    quad = NF // 2
    next_marks = white_ref[FIRST * rows :, :LANES].astype(F32)[:segs, :rows].astype(BF)

    def body(i, carry):
        at = pl.ds(pl.multiple_of(i * step, step), step)
        to = pl.ds(i * (step // per), step // per)
        hot = next_ref[at, :]
        for k, part in enumerate(add_segments(at, FIRST, 0, white_ref, source_ref, hot, sum_ref)):
            out_ref[at, k * quad : (k + 1) * quad] = part
        both = source_mark_ref[at, :] * (own_mark_ref[at, :] + dot_across(hot, next_marks))
        shared = jnp.broadcast_to(jnp.sum(both, axis=1, keepdims=True), (step, LANES)).reshape(-1, per, LANES)
        tail = shared[:, :8, :]
        lane = lax.broadcasted_iota(jnp.int32, tail.shape, 2)
        for k in range(1, per // 8):
            tail = jnp.where(lane >= k * 8 * LANES // per, shared[:, 8 * k : 8 * k + 8, :], tail)
        tail_ref[to, :, :] = tail
        return carry

    lax.fori_loop(0, pairs // step, body, 0)


def late_kernel(step, white_ref, source_ref, next_ref, sum_ref, tail_ref, out_ref):
    pairs = sum_ref.shape[0]
    per = pairs // out_ref.shape[0]
    late = source_ref.shape[0] - FIRST
    out_ref[:, 2 * NF // LANES * per :, :] = tail_ref[...].astype(BF)

    def body(i, carry):
        at = pl.ds(pl.multiple_of(i * step, step), step)
        to = pl.ds(i * (step // per), step // per)
        for k, part in enumerate(
            add_segments(at, late, FIRST, white_ref, source_ref, next_ref[at, :], sum_ref)
        ):
            out_ref[to, k * per : (k + 1) * per, :] = part.astype(BF).reshape(-1, per, LANES)
        return carry

    lax.fori_loop(0, pairs // step, body, 0)


def lags_kernel(parts, per, x_ref, high_ref, low_ref, out_ref):
    dests, length, _ = x_ref.shape
    blocks = 2 * NF // LANES
    total = jnp.sum(x_ref[...].astype(F32).reshape(dests // parts, parts, length, LANES), axis=1)
    scale = 1.0 / jnp.maximum(total[:, blocks * per :, :], 1.0)
    scale = jnp.concatenate(
        [scale[:, :, k * 8 * LANES // per :][:, :, :1] for k in range(per // 8)], axis=1
    )
    stacked = jnp.concatenate(
        [
            (total[:, k * per : (k + 1) * per, :] * scale).reshape(-1, LANES)
            for k in range(blocks)
        ],
        axis=1,
    )
    coarse, fine = halves(stacked)
    traces = dot(coarse, high_ref[...]) + dot(fine, high_ref[...]) + dot(coarse, low_ref[...])
    out_ref[...] = traces.reshape(out_ref.shape)


def call(kernel, shape, args, specs, scratch=(), mib=24):
    return pl.pallas_call(
        kernel,
        out_shape=shape,
        in_specs=specs,
        out_specs=[VMEM] * len(shape),
        scratch_shapes=list(scratch),
        compiler_params=pltpu.CompilerParams(vmem_limit_bytes=mib << 20),
    )(*args)


def local(records, gap_mask, pair_list, pair_counts):
    rows, segs, span = records.shape
    owners, slots = pair_list.shape[2:]
    chan, nbr = lax.axis_size("chan"), lax.axis_size("nbr")
    per = slots // nbr
    pairs = owners * slots
    step = min(STEP, pairs)
    width = 2 * NF
    back = [(i, i - 1) for i in range(1, chan)]
    shape = jax.ShapeDtypeStruct
    tables = forward_tables(span)
    inputs = (jnp.transpose(records, (1, 0, 2)), gap_mask.T, jnp.asarray(tables), jnp.asarray(taper()))
    extra = -(-segs // 16) * 16
    early, late = call(
        whiten_kernel,
        [shape((FIRST * rows + extra, width), BF), shape(((segs - FIRST) * rows, width), BF)],
        [pltpu.with_memory_space_constraint(v, pltpu.HBM) for v in inputs],
        [HBM] * 4,
        [
            pltpu.VMEM((segs, rows, span), F32),
            pltpu.VMEM((segs, rows), jnp.int32),
            pltpu.VMEM(tables.shape, BF),
            pltpu.VMEM((1, width), F32),
            pltpu.VMEM((extra, width), F32),
            pltpu.SemaphoreType.DMA((5,)),
        ],
        mib=32,
    )
    next_early = lax.ppermute(early, "chan", back)
    next_late = lax.ppermute(late, "chan", back)
    source, sums, hot, source_marks, own_marks = call(
        functools.partial(sources_kernel, step),
        [
            shape((segs, pairs, width), BF),
            shape((pairs, width), F32),
            shape((pairs, rows), BF),
            shape((pairs, segs), F32),
            shape((pairs, segs), F32),
        ],
        (early, late, gap_mask.T, pair_list, pair_counts),
        [VMEM] * 4 + [SMEM],
        [pltpu.VMEM((pairs, rows), BF), pltpu.VMEM((pairs, rows), BF)],
        mib=40,
    )
    sums, tail = call(
        functools.partial(early_kernel, step),
        [shape((pairs, width), F32), shape((chan * nbr, 8, LANES), F32)],
        (next_early, source, hot, sums, source_marks, own_marks),
        [VMEM] * 6,
        mib=40,
    )
    (cross,) = call(
        functools.partial(late_kernel, step),
        [shape((chan * nbr, width // LANES * per + 8, LANES), BF)],
        (next_late, source, hot, sums, tail),
        [VMEM] * 5,
        mib=40,
    )
    arrived = lax.all_to_all(cross, ("chan", "nbr"), split_axis=0, concat_axis=0, tiled=True)
    high, low = inverse_tables(span)
    (traces,) = call(
        functools.partial(lags_kernel, nbr, per),
        [shape((chan, per, NLAG), F32)],
        (arrived, jnp.asarray(high), jnp.asarray(low)),
        [VMEM] * 3,
    )
    return traces[None]


def solution(mesh):
    return jax.shard_map(
        local,
        mesh=mesh,
        in_specs=(
            P("chan", "nbr", None),
            P("chan", "nbr"),
            P("chan", None, None, None),
            P("chan", None),
        ),
        out_specs=P("chan", None, "nbr", None),
        check_vma=False,
    )
```

```python
import functools
import math

import jax
import jax.numpy as jnp
import ml_dtypes
import numpy as np
from jax import lax
from jax.experimental import pallas as pl
from jax.experimental.pallas import tpu as pltpu
from jax.sharding import PartitionSpec as P

NF = 256
NLAG = 1024
LANES = 128
BF = jnp.bfloat16
F32 = jnp.float32
VMEM = pl.BlockSpec(memory_space=pltpu.VMEM)
HBM = pl.BlockSpec(memory_space=pltpu.HBM)
SMEM = pl.BlockSpec(memory_space=pltpu.SMEM)

EVEN, ODD = np.arange(2, NF + 1, 2), np.arange(1, NF + 1, 2)
FIRST = 4
STEP = 512


def two_parts(table):
    high = table.astype(ml_dtypes.bfloat16)
    return high, (table - high.astype(np.float64)).astype(ml_dtypes.bfloat16)


def forward_tables(span):
    clock = np.arange(span // 2)[:, None]
    parts = []
    for bins in (EVEN, ODD):
        angle = (clock * bins[None, :] % span) * (2.0 * math.pi / span)
        table = np.concatenate([np.cos(angle), -np.sin(angle)], axis=1)
        parts.append(np.concatenate(two_parts(table), axis=0))
    return np.stack(parts)


def inverse_tables(span):
    lag = np.arange(NLAG)[None, :] - NLAG // 2
    rows = []
    for bins in (EVEN, ODD):
        angle = (bins[:, None] * lag % span) * (2.0 * math.pi / span)
        rows += [np.cos(angle), -np.sin(angle)]
    return two_parts(np.concatenate(rows, axis=0))


def taper():
    window = np.sin(math.pi * np.concatenate([EVEN, EVEN, ODD, ODD]) / (NF + 1.0))
    return window[None, :].astype(np.float32)


def halves(value):
    high = value.astype(BF)
    return high, (value - high.astype(F32)).astype(BF)


def dot(a, b):
    return jnp.dot(a, b, preferred_element_type=F32)


def dot_across(a, b):
    return lax.dot_general(a, b, (((1,), (1,)), ((), ())), preferred_element_type=F32)


def as_column(row):
    size = row.shape[1]
    shape = (size, size)
    same = lax.broadcasted_iota(jnp.int32, shape, 0) == lax.broadcasted_iota(jnp.int32, shape, 1)
    return jnp.sum(jnp.where(same, row, 0.0), axis=1, keepdims=True)


def whiten(x_ref, flags, table_ref, taper_ref):
    segs, rows, span = x_ref.shape
    half = span // 2
    low = x_ref[:, :, :half].reshape(segs * rows, half)
    high = x_ref[:, :, half:].reshape(segs * rows, half)
    found = []
    for i, folded in enumerate((low + high, low - high)):
        coarse, fine = halves(folded)
        found.append(
            dot(fine, table_ref[i, :half, :]) + dot(jnp.concatenate([coarse, coarse], axis=1), table_ref[i])
        )
    even, odd = found
    energy = jnp.sum(even * even + odd * odd, axis=1, keepdims=True) * (0.5 / NF)
    factor = flags / jnp.sqrt(energy + 1e-05)
    return [
        (part * factor * taper_ref[:, i * NF : (i + 1) * NF]).astype(BF) for i, part in enumerate(found)
    ]


def first_kernel(x_hbm, mark_hbm, table_hbm, taper_hbm, early_ref, rest, table, window, factors, x, mark, row, sem):
    total, rows, _ = x_hbm.shape
    early = x.shape[0]
    small = [
        pltpu.make_async_copy(mark_hbm, mark, sem.at[0]),
        pltpu.make_async_copy(taper_hbm, window, sem.at[1]),
    ]
    large = [
        pltpu.make_async_copy(table_hbm, table, sem.at[2]),
        pltpu.make_async_copy(x_hbm.at[pl.ds(0, early)], x, sem.at[3]),
        pltpu.make_async_copy(x_hbm.at[pl.ds(early, total - early)], rest, sem.at[4]),
    ]
    for copy in small + large[:2]:
        copy.start()
    for copy in small:
        copy.wait()
    large[2].start()
    flags = [as_column(mark[s : s + 1, :].astype(F32)) for s in range(total)]
    factors[...] = jnp.concatenate(flags[early:], axis=0)
    row[...] = jnp.zeros(row.shape, F32)
    row[:total, :rows] = mark[...].astype(F32)
    early_ref[early * rows :, :] = row[...].astype(BF)
    large[0].wait()
    large[1].wait()
    for i, white in enumerate(whiten(x, jnp.concatenate(flags[:early], axis=0), table, window)):
        early_ref[: early * rows, i * NF : (i + 1) * NF] = white
    large[2].wait()


def second_kernel(x_ref, table_ref, window_ref, factor_ref, late_ref):
    for i, white in enumerate(whiten(x_ref, factor_ref[...], table_ref, window_ref)):
        late_ref[:, i * NF : (i + 1) * NF] = white


def add_products(real, imag, a, b):
    quad = NF // 2
    ar, ai, br, bi = a[:, :quad], a[:, quad:], b[:, :quad], b[:, quad:]
    return real + (ar * br + ai * bi), imag + (ai * br - ar * bi)


def sources_kernel(
    step, early_ref, late_ref, mark_ref, list_ref, count_ref,
    source_ref, sum_ref, next_ref, source_mark_ref, own_mark_ref, first, own,
):
    segs, rows = mark_ref.shape
    owners, slots = list_ref.shape[2:]
    quad = NF // 2
    anchor = lax.axis_index("chan") * rows
    spots = lax.broadcasted_iota(jnp.int32, (slots, rows), 1).astype(F32)
    for o in range(owners):
        live = lax.broadcasted_iota(jnp.int32, (1, slots), 1) < count_ref[0, o]
        where = slice(o * slots, (o + 1) * slots)
        column = as_column(jnp.where(live, list_ref[0, 0, o : o + 1, :] - anchor, -1).astype(F32))
        first[where, :] = (spots == column).astype(BF)
        column = as_column((list_ref[0, 1, o : o + 1, :] - anchor).astype(F32))
        own[where, :] = (spots == column).astype(BF)
        next_ref[where, :] = (spots == column - rows).astype(BF)
    marks = mark_ref[...].astype(BF)

    def body(i, carry):
        at = pl.ds(pl.multiple_of(i * step, step), step)
        a_hot, b_hot = first[at, :], own[at, :]
        source_mark_ref[at, :] = dot_across(a_hot, marks)
        own_mark_ref[at, :] = dot_across(b_hot, marks)
        for h in range(2):
            columns = slice(h * NF, (h + 1) * NF)
            real = imag = jnp.zeros((step, quad), F32)
            for s in range(segs):
                ref, base = (early_ref, s) if s < FIRST else (late_ref, s - FIRST)
                white = ref[base * rows : (base + 1) * rows, columns]
                a = dot(a_hot, white)
                source_ref[s, at, columns] = a.astype(BF)
                real, imag = add_products(real, imag, a, dot(b_hot, white))
            sum_ref[at, h * NF : h * NF + quad] = real
            sum_ref[at, h * NF + quad : (h + 1) * NF] = imag
        return carry

    lax.fori_loop(0, owners * slots // step, body, 0)


def add_segments(at, segs, base, white_ref, source_ref, hot, sums):
    quad = NF // 2
    rows = hot.shape[1]
    result = []
    for h in range(2):
        columns = slice(h * NF, (h + 1) * NF)
        real, imag = sums[at, h * NF : h * NF + quad], sums[at, h * NF + quad : (h + 1) * NF]
        for s in range(segs):
            a = source_ref[base + s, at, columns].astype(F32)
            real, imag = add_products(real, imag, a, dot(hot, white_ref[s * rows : (s + 1) * rows, columns]))
        result += [real, imag]
    return result


def early_kernel(
    step, white_ref, source_ref, next_ref, sum_ref, source_mark_ref, own_mark_ref, out_ref, tail_ref
):
    pairs, rows = next_ref.shape
    segs = source_mark_ref.shape[1]
    per = pairs // tail_ref.shape[0]
    quad = NF // 2
    next_marks = white_ref[FIRST * rows :, :LANES].astype(F32)[:segs, :rows].astype(BF)

    def body(i, carry):
        at = pl.ds(pl.multiple_of(i * step, step), step)
        to = pl.ds(i * (step // per), step // per)
        hot = next_ref[at, :]
        for k, part in enumerate(add_segments(at, FIRST, 0, white_ref, source_ref, hot, sum_ref)):
            out_ref[at, k * quad : (k + 1) * quad] = part
        both = source_mark_ref[at, :] * (own_mark_ref[at, :] + dot_across(hot, next_marks))
        shared = jnp.broadcast_to(jnp.sum(both, axis=1, keepdims=True), (step, LANES)).reshape(-1, per, LANES)
        tail = shared[:, :8, :]
        lane = lax.broadcasted_iota(jnp.int32, tail.shape, 2)
        for k in range(1, per // 8):
            tail = jnp.where(lane >= k * 8 * LANES // per, shared[:, 8 * k : 8 * k + 8, :], tail)
        tail_ref[to, :, :] = tail
        return carry

    lax.fori_loop(0, pairs // step, body, 0)


def late_kernel(step, white_ref, source_ref, next_ref, sum_ref, tail_ref, out_ref):
    pairs = sum_ref.shape[0]
    per = pairs // out_ref.shape[0]
    late = source_ref.shape[0] - FIRST
    out_ref[:, 2 * NF // LANES * per :, :] = tail_ref[...].astype(BF)

    def body(i, carry):
        at = pl.ds(pl.multiple_of(i * step, step), step)
        to = pl.ds(i * (step // per), step // per)
        for k, part in enumerate(
            add_segments(at, late, FIRST, white_ref, source_ref, next_ref[at, :], sum_ref)
        ):
            out_ref[to, k * per : (k + 1) * per, :] = part.astype(BF).reshape(-1, per, LANES)
        return carry

    lax.fori_loop(0, pairs // step, body, 0)


def lags_kernel(parts, per, x_ref, high_ref, low_ref, out_ref):
    dests, length, _ = x_ref.shape
    blocks = 2 * NF // LANES
    total = jnp.sum(x_ref[...].astype(F32).reshape(dests // parts, parts, length, LANES), axis=1)
    scale = 1.0 / jnp.maximum(total[:, blocks * per :, :], 1.0)
    scale = jnp.concatenate(
        [scale[:, :, k * 8 * LANES // per :][:, :, :1] for k in range(per // 8)], axis=1
    )
    stacked = jnp.concatenate(
        [
            (total[:, k * per : (k + 1) * per, :] * scale).reshape(-1, LANES)
            for k in range(blocks)
        ],
        axis=1,
    )
    coarse, fine = halves(stacked)
    traces = dot(coarse, high_ref[...]) + dot(fine, high_ref[...]) + dot(coarse, low_ref[...])
    out_ref[...] = traces.reshape(out_ref.shape)


def call(kernel, shape, args, specs, scratch=(), mib=24):
    return pl.pallas_call(
        kernel,
        out_shape=shape,
        in_specs=specs,
        out_specs=[VMEM] * len(shape),
        scratch_shapes=list(scratch),
        compiler_params=pltpu.CompilerParams(vmem_limit_bytes=mib << 20),
    )(*args)


def local(records, gap_mask, pair_list, pair_counts):
    rows, segs, span = records.shape
    owners, slots = pair_list.shape[2:]
    chan, nbr = lax.axis_size("chan"), lax.axis_size("nbr")
    per = slots // nbr
    pairs = owners * slots
    step = min(STEP, pairs)
    width = 2 * NF
    back = [(i, i - 1) for i in range(1, chan)]
    shape = jax.ShapeDtypeStruct
    tables = forward_tables(span)
    inputs = (jnp.transpose(records, (1, 0, 2)), gap_mask.T, jnp.asarray(tables), jnp.asarray(taper()))
    extra = -(-segs // 16) * 16
    early, rest, table, window, factors = call(
        first_kernel,
        [
            shape((FIRST * rows + extra, width), BF),
            shape((segs - FIRST, rows, span), F32),
            shape(tables.shape, BF),
            shape((1, width), F32),
            shape(((segs - FIRST) * rows, 1), F32),
        ],
        [pltpu.with_memory_space_constraint(v, pltpu.HBM) for v in inputs],
        [HBM] * 4,
        [
            pltpu.VMEM((FIRST, rows, span), F32),
            pltpu.VMEM((segs, rows), jnp.int32),
            pltpu.VMEM((extra, width), F32),
            pltpu.SemaphoreType.DMA((5,)),
        ],
        mib=32,
    )
    (late,) = call(
        second_kernel,
        [shape(((segs - FIRST) * rows, width), BF)],
        (rest, table, window, factors),
        [VMEM] * 4,
    )
    next_early = lax.ppermute(early, "chan", back)
    next_late = lax.ppermute(late, "chan", back)
    source, sums, hot, source_marks, own_marks = call(
        functools.partial(sources_kernel, step),
        [
            shape((segs, pairs, width), BF),
            shape((pairs, width), F32),
            shape((pairs, rows), BF),
            shape((pairs, segs), F32),
            shape((pairs, segs), F32),
        ],
        (early, late, gap_mask.T, pair_list, pair_counts),
        [VMEM] * 4 + [SMEM],
        [pltpu.VMEM((pairs, rows), BF), pltpu.VMEM((pairs, rows), BF)],
        mib=40,
    )
    sums, tail = call(
        functools.partial(early_kernel, step),
        [shape((pairs, width), F32), shape((chan * nbr, 8, LANES), F32)],
        (next_early, source, hot, sums, source_marks, own_marks),
        [VMEM] * 6,
        mib=40,
    )
    (cross,) = call(
        functools.partial(late_kernel, step),
        [shape((chan * nbr, width // LANES * per + 8, LANES), BF)],
        (next_late, source, hot, sums, tail),
        [VMEM] * 5,
        mib=40,
    )
    arrived = lax.all_to_all(cross, ("chan", "nbr"), split_axis=0, concat_axis=0, tiled=True)
    high, low = inverse_tables(span)
    (traces,) = call(
        functools.partial(lags_kernel, nbr, per),
        [shape((chan, per, NLAG), F32)],
        (arrived, jnp.asarray(high), jnp.asarray(low)),
        [VMEM] * 3,
    )
    return traces[None]


def solution(mesh):
    return jax.shard_map(
        local,
        mesh=mesh,
        in_specs=(
            P("chan", "nbr", None),
            P("chan", "nbr"),
            P("chan", None, None, None),
            P("chan", None),
        ),
        out_specs=P("chan", None, "nbr", None),
        check_vma=False,
    )
```

```python
import functools
import math

import jax
import jax.numpy as jnp
import ml_dtypes
import numpy as np
from jax import lax
from jax.experimental import pallas as pl
from jax.experimental.pallas import tpu as pltpu
from jax.sharding import PartitionSpec as P

NF = 256
NLAG = 1024
LANES = 128
BF = jnp.bfloat16
F32 = jnp.float32
VMEM = pl.BlockSpec(memory_space=pltpu.VMEM)
HBM = pl.BlockSpec(memory_space=pltpu.HBM)
SMEM = pl.BlockSpec(memory_space=pltpu.SMEM)

EVEN, ODD = np.arange(2, NF + 1, 2), np.arange(1, NF + 1, 2)
FIRST = 4
STEP = 512
HALVES = 2


def two_parts(table):
    high = table.astype(ml_dtypes.bfloat16)
    return high, (table - high.astype(np.float64)).astype(ml_dtypes.bfloat16)


def forward_tables(span):
    clock = np.arange(span // 2)[:, None]
    parts = []
    for bins in (EVEN, ODD):
        angle = (clock * bins[None, :] % span) * (2.0 * math.pi / span)
        table = np.concatenate([np.cos(angle), -np.sin(angle)], axis=1)
        parts.append(np.concatenate(two_parts(table), axis=0))
    return np.stack(parts)


def inverse_tables(span):
    lag = np.arange(NLAG)[None, :] - NLAG // 2
    rows = []
    for bins in (EVEN, ODD):
        angle = (bins[:, None] * lag % span) * (2.0 * math.pi / span)
        rows += [np.cos(angle), -np.sin(angle)]
    return two_parts(np.concatenate(rows, axis=0))


def taper():
    window = np.sin(math.pi * np.concatenate([EVEN, EVEN, ODD, ODD]) / (NF + 1.0))
    return window[None, :].astype(np.float32)


def halves(value):
    high = value.astype(BF)
    return high, (value - high.astype(F32)).astype(BF)


def dot(a, b):
    return jnp.dot(a, b, preferred_element_type=F32)


def dot_across(a, b):
    return lax.dot_general(a, b, (((1,), (1,)), ((), ())), preferred_element_type=F32)


def as_column(row):
    size = row.shape[1]
    shape = (size, size)
    same = lax.broadcasted_iota(jnp.int32, shape, 0) == lax.broadcasted_iota(jnp.int32, shape, 1)
    return jnp.sum(jnp.where(same, row, 0.0), axis=1, keepdims=True)


def whiten(x_ref, flags, table_ref, taper_ref):
    segs, rows, span = x_ref.shape
    half = span // 2
    low = x_ref[:, :, :half].reshape(segs * rows, half)
    high = x_ref[:, :, half:].reshape(segs * rows, half)
    found = []
    for i, folded in enumerate((low + high, low - high)):
        coarse, fine = halves(folded)
        found.append(
            dot(fine, table_ref[i, :half, :]) + dot(jnp.concatenate([coarse, coarse], axis=1), table_ref[i])
        )
    even, odd = found
    energy = jnp.sum(even * even + odd * odd, axis=1, keepdims=True) * (0.5 / NF)
    factor = flags / jnp.sqrt(energy + 1e-05)
    return [
        (part * factor * taper_ref[:, i * NF : (i + 1) * NF]).astype(BF) for i, part in enumerate(found)
    ]


def first_kernel(x_hbm, mark_hbm, table_hbm, taper_hbm, early_ref, rest, table, window, factors, x, mark, row, sem):
    total, rows, _ = x_hbm.shape
    early = x.shape[0]
    small = [
        pltpu.make_async_copy(mark_hbm, mark, sem.at[0]),
        pltpu.make_async_copy(taper_hbm, window, sem.at[1]),
    ]
    large = [
        pltpu.make_async_copy(table_hbm, table, sem.at[2]),
        pltpu.make_async_copy(x_hbm.at[pl.ds(0, early)], x, sem.at[3]),
        pltpu.make_async_copy(x_hbm.at[pl.ds(early, total - early)], rest, sem.at[4]),
    ]
    for copy in small + large[:2]:
        copy.start()
    for copy in small:
        copy.wait()
    large[2].start()
    flags = [as_column(mark[s : s + 1, :].astype(F32)) for s in range(total)]
    factors[...] = jnp.concatenate(flags[early:], axis=0)
    row[...] = jnp.zeros(row.shape, F32)
    row[:total, :rows] = mark[...].astype(F32)
    early_ref[early * rows :, :] = row[...].astype(BF)
    large[0].wait()
    large[1].wait()
    for i, white in enumerate(whiten(x, jnp.concatenate(flags[:early], axis=0), table, window)):
        early_ref[: early * rows, i * NF : (i + 1) * NF] = white
    large[2].wait()


def second_kernel(x_ref, table_ref, window_ref, factor_ref, late_ref):
    for i, white in enumerate(whiten(x_ref, factor_ref[...], table_ref, window_ref)):
        late_ref[:, i * NF : (i + 1) * NF] = white


def add_products(real, imag, a, b):
    quad = NF // 2
    ar, ai, br, bi = a[:, :quad], a[:, quad:], b[:, :quad], b[:, quad:]
    return real + (ar * br + ai * bi), imag + (ai * br - ar * bi)


def sources_kernel(
    step, early_ref, late_ref, mark_ref, list_ref, count_ref,
    source_ref, sum_ref, next_ref, source_mark_ref, own_mark_ref, first, own,
):
    segs, rows = mark_ref.shape
    owners, slots = list_ref.shape[2:]
    quad = NF // 2
    anchor = lax.axis_index("chan") * rows
    spots = lax.broadcasted_iota(jnp.int32, (slots, rows), 1).astype(F32)
    for o in range(owners):
        live = lax.broadcasted_iota(jnp.int32, (1, slots), 1) < count_ref[0, o]
        where = slice(o * slots, (o + 1) * slots)
        column = as_column(jnp.where(live, list_ref[0, 0, o : o + 1, :] - anchor, -1).astype(F32))
        first[where, :] = (spots == column).astype(BF)
        column = as_column((list_ref[0, 1, o : o + 1, :] - anchor).astype(F32))
        own[where, :] = (spots == column).astype(BF)
        next_ref[where, :] = (spots == column - rows).astype(BF)
    marks = mark_ref[...].astype(BF)

    def body(i, carry):
        at = pl.ds(pl.multiple_of(i * step, step), step)
        a_hot, b_hot = first[at, :], own[at, :]
        source_mark_ref[at, :] = dot_across(a_hot, marks)
        own_mark_ref[at, :] = dot_across(b_hot, marks)
        for h in range(2):
            columns = slice(h * NF, (h + 1) * NF)
            real = imag = jnp.zeros((step, quad), F32)
            for s in range(segs):
                ref, base = (early_ref, s) if s < FIRST else (late_ref, s - FIRST)
                white = ref[base * rows : (base + 1) * rows, columns]
                a = dot(a_hot, white)
                source_ref[s, at, columns] = a
                real, imag = add_products(real, imag, a, dot(b_hot, white))
            sum_ref[at, h * NF : h * NF + quad] = real
            sum_ref[at, h * NF + quad : (h + 1) * NF] = imag
        return carry

    lax.fori_loop(0, owners * slots // step, body, 0)


def add_segments(at, segs, base, white_ref, source_ref, hot, sums):
    quad = NF // 2
    rows = hot.shape[1]
    result = []
    for h in range(2):
        columns = slice(h * NF, (h + 1) * NF)
        real, imag = sums[at, h * NF : h * NF + quad], sums[at, h * NF + quad : (h + 1) * NF]
        for s in range(segs):
            a = source_ref[base + s, at, columns]
            real, imag = add_products(real, imag, a, dot(hot, white_ref[s * rows : (s + 1) * rows, columns]))
        result += [real, imag]
    return result


def early_kernel(
    step, white_ref, source_ref, next_ref, sum_ref, source_mark_ref, own_mark_ref, out_ref, tail_ref
):
    pairs, rows = next_ref.shape
    segs = source_mark_ref.shape[1]
    per = pairs // tail_ref.shape[0]
    quad = NF // 2
    next_marks = white_ref[FIRST * rows :, :LANES].astype(F32)[:segs, :rows].astype(BF)

    def body(i, carry):
        at = pl.ds(pl.multiple_of(i * step, step), step)
        to = pl.ds(i * (step // per), step // per)
        hot = next_ref[at, :]
        for k, part in enumerate(add_segments(at, FIRST, 0, white_ref, source_ref, hot, sum_ref)):
            out_ref[at, k * quad : (k + 1) * quad] = part
        both = source_mark_ref[at, :] * (own_mark_ref[at, :] + dot_across(hot, next_marks))
        shared = jnp.broadcast_to(jnp.sum(both, axis=1, keepdims=True), (step, LANES)).reshape(-1, per, LANES)
        tail = shared[:, :8, :]
        lane = lax.broadcasted_iota(jnp.int32, tail.shape, 2)
        for k in range(1, per // 8):
            tail = jnp.where(lane >= k * 8 * LANES // per, shared[:, 8 * k : 8 * k + 8, :], tail)
        tail_ref[to, :, :] = tail
        return carry

    lax.fori_loop(0, pairs // step, body, 0)


def late_kernel(step, white_ref, source_ref, next_ref, sum_ref, tail_ref, out_ref):
    pairs = sum_ref.shape[0]
    per = pairs // out_ref.shape[0]
    late = source_ref.shape[0] - FIRST
    out_ref[:, 2 * NF // LANES * per :, :] = tail_ref[...].astype(BF)

    def body(i, carry):
        at = pl.ds(pl.multiple_of(i * step, step), step)
        to = pl.ds(i * (step // per), step // per)
        for k, part in enumerate(
            add_segments(at, late, FIRST, white_ref, source_ref, next_ref[at, :], sum_ref)
        ):
            out_ref[to, k * per : (k + 1) * per, :] = part.astype(BF).reshape(-1, per, LANES)
        return carry

    lax.fori_loop(0, pairs // step, body, 0)


def lags_kernel(parts, per, x_ref, high_ref, low_ref, out_hbm, held, sem):
    dests, length, _ = x_ref.shape
    blocks = 2 * NF // LANES
    total = jnp.sum(x_ref[...].astype(F32).reshape(dests // parts, parts, length, LANES), axis=1)
    scale = 1.0 / jnp.maximum(total[:, blocks * per :, :], 1.0)
    scale = jnp.concatenate(
        [scale[:, :, k * 8 * LANES // per :][:, :, :1] for k in range(per // 8)], axis=1
    )
    stacked = jnp.concatenate(
        [
            (total[:, k * per : (k + 1) * per, :] * scale).reshape(-1, LANES)
            for k in range(blocks)
        ],
        axis=1,
    )
    coarse, fine = halves(stacked)
    both = jnp.concatenate([coarse, fine], axis=0)
    count = stacked.shape[0]
    copies = []
    for k in range(HALVES):
        columns = slice(k * NLAG // HALVES, (k + 1) * NLAG // HALVES)
        product = dot(both, high_ref[:, columns])
        traces = product[:count] + product[count:] + dot(coarse, low_ref[:, columns])
        held[:, :, columns] = traces.reshape(held.shape[0], held.shape[1], -1)
        part = pl.ds(k * NLAG // HALVES, NLAG // HALVES)
        copies.append(pltpu.make_async_copy(held.at[:, :, part], out_hbm.at[:, :, part], sem.at[k]))
        copies[-1].start()
    for copy in copies:
        copy.wait()


def call(kernel, shape, args, specs, scratch=(), mib=24, out=VMEM):
    return pl.pallas_call(
        kernel,
        out_shape=shape,
        in_specs=specs,
        out_specs=[out] * len(shape),
        scratch_shapes=list(scratch),
        compiler_params=pltpu.CompilerParams(vmem_limit_bytes=mib << 20),
    )(*args)


def local(records, gap_mask, pair_list, pair_counts):
    rows, segs, span = records.shape
    owners, slots = pair_list.shape[2:]
    chan, nbr = lax.axis_size("chan"), lax.axis_size("nbr")
    per = slots // nbr
    pairs = owners * slots
    step = min(STEP, pairs)
    width = 2 * NF
    back = [(i, i - 1) for i in range(1, chan)]
    shape = jax.ShapeDtypeStruct
    tables = forward_tables(span)
    inputs = (jnp.transpose(records, (1, 0, 2)), gap_mask.T, jnp.asarray(tables), jnp.asarray(taper()))
    extra = -(-segs // 16) * 16
    early, rest, table, window, factors = call(
        first_kernel,
        [
            shape((FIRST * rows + extra, width), BF),
            shape((segs - FIRST, rows, span), F32),
            shape(tables.shape, BF),
            shape((1, width), F32),
            shape(((segs - FIRST) * rows, 1), F32),
        ],
        [pltpu.with_memory_space_constraint(v, pltpu.HBM) for v in inputs],
        [HBM] * 4,
        [
            pltpu.VMEM((FIRST, rows, span), F32),
            pltpu.VMEM((segs, rows), jnp.int32),
            pltpu.VMEM((extra, width), F32),
            pltpu.SemaphoreType.DMA((5,)),
        ],
        mib=32,
    )
    (late,) = call(
        second_kernel,
        [shape(((segs - FIRST) * rows, width), BF)],
        (rest, table, window, factors),
        [VMEM] * 4,
    )
    next_early = lax.ppermute(early, "chan", back)
    next_late = lax.ppermute(late, "chan", back)
    source, sums, hot, source_marks, own_marks = call(
        functools.partial(sources_kernel, step),
        [
            shape((segs, pairs, width), F32),
            shape((pairs, width), F32),
            shape((pairs, rows), BF),
            shape((pairs, segs), F32),
            shape((pairs, segs), F32),
        ],
        (early, late, gap_mask.T, pair_list, pair_counts),
        [VMEM] * 4 + [SMEM],
        [pltpu.VMEM((pairs, rows), BF), pltpu.VMEM((pairs, rows), BF)],
        mib=40,
    )
    sums, tail = call(
        functools.partial(early_kernel, step),
        [shape((pairs, width), F32), shape((chan * nbr, 8, LANES), F32)],
        (next_early, source, hot, sums, source_marks, own_marks),
        [VMEM] * 6,
        mib=40,
    )
    (cross,) = call(
        functools.partial(late_kernel, step),
        [shape((chan * nbr, width // LANES * per + 8, LANES), BF)],
        (next_late, source, hot, sums, tail),
        [VMEM] * 5,
        mib=40,
    )
    arrived = lax.all_to_all(cross, ("chan", "nbr"), split_axis=0, concat_axis=0, tiled=True)
    high, low = inverse_tables(span)
    (traces,) = call(
        functools.partial(lags_kernel, nbr, per),
        [shape((chan, per, NLAG), F32)],
        (arrived, jnp.asarray(high), jnp.asarray(low)),
        [VMEM] * 3,
        [pltpu.VMEM((chan, per, NLAG), F32), pltpu.SemaphoreType.DMA((HALVES,))],
        out=HBM,
    )
    return traces[None]


def solution(mesh):
    return jax.shard_map(
        local,
        mesh=mesh,
        in_specs=(
            P("chan", "nbr", None),
            P("chan", "nbr"),
            P("chan", None, None, None),
            P("chan", None),
        ),
        out_specs=P("chan", None, "nbr", None),
        check_vma=False,
    )
```

```python
import functools
import math

import jax
import jax.numpy as jnp
import ml_dtypes
import numpy as np
from jax import lax
from jax.experimental import pallas as pl
from jax.experimental.pallas import tpu as pltpu
from jax.sharding import PartitionSpec as P

NF = 256
NLAG = 1024
LANES = 128
BF = jnp.bfloat16
F32 = jnp.float32
VMEM = pl.BlockSpec(memory_space=pltpu.VMEM)
HBM = pl.BlockSpec(memory_space=pltpu.HBM)
SMEM = pl.BlockSpec(memory_space=pltpu.SMEM)

EVEN, ODD = np.arange(2, NF + 1, 2), np.arange(1, NF + 1, 2)
FIRST = 4
STEP = 512
HALVES = 2


def two_parts(table):
    high = table.astype(ml_dtypes.bfloat16)
    return high, (table - high.astype(np.float64)).astype(ml_dtypes.bfloat16)


def forward_tables(span):
    clock = np.arange(span // 2)[:, None]
    parts = []
    for bins in (EVEN, ODD):
        angle = (clock * bins[None, :] % span) * (2.0 * math.pi / span)
        table = np.concatenate([np.cos(angle), -np.sin(angle)], axis=1)
        parts.append(np.concatenate(two_parts(table), axis=0))
    return np.stack(parts)


def inverse_tables(span):
    lag = np.arange(NLAG)[None, :] - NLAG // 2
    rows = []
    for bins in (EVEN, ODD):
        angle = (bins[:, None] * lag % span) * (2.0 * math.pi / span)
        rows += [np.cos(angle), -np.sin(angle)]
    return two_parts(np.concatenate(rows, axis=0))


def taper():
    window = np.sin(math.pi * np.concatenate([EVEN, EVEN, ODD, ODD]) / (NF + 1.0))
    return window[None, :].astype(np.float32)


def halves(value):
    high = value.astype(BF)
    return high, (value - high.astype(F32)).astype(BF)


def dot(a, b):
    return jnp.dot(a, b, preferred_element_type=F32)


def dot_across(a, b):
    return lax.dot_general(a, b, (((1,), (1,)), ((), ())), preferred_element_type=F32)


def as_column(row):
    size = row.shape[1]
    shape = (size, size)
    same = lax.broadcasted_iota(jnp.int32, shape, 0) == lax.broadcasted_iota(jnp.int32, shape, 1)
    return jnp.sum(jnp.where(same, row, 0.0), axis=1, keepdims=True)


def whiten(x_ref, flags, table_ref, taper_ref):
    segs, rows, span = x_ref.shape
    half = span // 2
    low = x_ref[:, :, :half].reshape(segs * rows, half)
    high = x_ref[:, :, half:].reshape(segs * rows, half)
    found = []
    for i, folded in enumerate((low + high, low - high)):
        coarse, fine = halves(folded)
        found.append(
            dot(fine, table_ref[i, :half, :]) + dot(jnp.concatenate([coarse, coarse], axis=1), table_ref[i])
        )
    even, odd = found
    energy = jnp.sum(even * even + odd * odd, axis=1, keepdims=True) * (0.5 / NF)
    factor = flags / jnp.sqrt(energy + 1e-05)
    return [
        part * factor * taper_ref[:, i * NF : (i + 1) * NF] for i, part in enumerate(found)
    ]


def share(found, keep_ref, give_ref, base):
    odd = lax.axis_index("nbr") % 2 == 1
    even_bins, odd_bins = found
    rows = even_bins.shape[0]
    keep_ref[base : base + rows, :] = jnp.where(odd, odd_bins, even_bins).astype(BF)
    give_ref[...] = jnp.where(odd, even_bins, odd_bins).astype(BF)


def first_kernel(
    x_hbm, mark_hbm, table_hbm, taper_hbm, keep_ref, give_ref, rest, table, window, factors, mark_rows, x, mark, row, sem
):
    total, rows, _ = x_hbm.shape
    early = x.shape[0]
    small = [
        pltpu.make_async_copy(mark_hbm, mark, sem.at[0]),
        pltpu.make_async_copy(taper_hbm, window, sem.at[1]),
    ]
    large = [
        pltpu.make_async_copy(table_hbm, table, sem.at[2]),
        pltpu.make_async_copy(x_hbm.at[pl.ds(0, early)], x, sem.at[3]),
        pltpu.make_async_copy(x_hbm.at[pl.ds(early, total - early)], rest, sem.at[4]),
    ]
    for copy in small + large[:2]:
        copy.start()
    for copy in small:
        copy.wait()
    large[2].start()
    flags = [as_column(mark[s : s + 1, :].astype(F32)) for s in range(total)]
    factors[...] = jnp.concatenate(flags[early:], axis=0)
    row[...] = jnp.zeros(row.shape, F32)
    row[:total, :rows] = mark[...].astype(F32)
    mark_rows[...] = row[...].astype(BF)
    large[0].wait()
    large[1].wait()
    found = whiten(x, jnp.concatenate(flags[:early], axis=0), table, window)
    share(found, keep_ref, give_ref, 0)
    large[2].wait()


def second_kernel(x_ref, table_ref, window_ref, factor_ref, early_ref, mark_rows, keep_ref, give_ref):
    found = whiten(x_ref, factor_ref[...], table_ref, window_ref)
    count = early_ref.shape[0]
    keep_ref[:count, :] = early_ref[...]
    share(found, keep_ref, give_ref, count)
    keep_ref[count + give_ref.shape[0] :, :] = mark_rows[...]


def add_products(real, imag, a, b):
    quad = NF // 2
    ar, ai, br, bi = a[:, :quad], a[:, quad:], b[:, :quad], b[:, quad:]
    return real + (ar * br + ai * bi), imag + (ai * br - ar * bi)


def first_terms(at, white_ref, segs, base, a_hot, b_hot, source_ref, real, imag):
    rows = a_hot.shape[1]
    for s in range(segs):
        white = white_ref[s * rows : (s + 1) * rows, :]
        a = dot(a_hot, white)
        source_ref[base + s, at, :] = a
        real, imag = add_products(real, imag, a, dot(b_hot, white))
    return real, imag


def more_terms(at, white_ref, segs, base, hot, source_ref, real, imag):
    rows = hot.shape[1]
    for s in range(segs):
        b = dot(hot, white_ref[s * rows : (s + 1) * rows, :])
        real, imag = add_products(real, imag, source_ref[base + s, at, :], b)
    return real, imag


def load_sums(sum_ref, at):
    return sum_ref[at, : NF // 2], sum_ref[at, NF // 2 :]


def store_sums(sum_ref, at, real, imag):
    sum_ref[at, : NF // 2] = real
    sum_ref[at, NF // 2 :] = imag


def in_steps(step, pairs, body):
    def run(i, carry):
        body(i, pl.ds(pl.multiple_of(i * step, step), step))
        return carry

    lax.fori_loop(0, pairs // step, run, 0)


def sources_kernel(
    step, white_ref, mark_ref, list_ref, count_ref,
    source_ref, sum_ref, first, own, next_ref, source_mark_ref, own_mark_ref,
):
    segs, rows = mark_ref.shape
    owners, slots = list_ref.shape[2:]
    anchor = lax.axis_index("chan") * rows
    spots = lax.broadcasted_iota(jnp.int32, (slots, rows), 1).astype(F32)
    for o in range(owners):
        live = lax.broadcasted_iota(jnp.int32, (1, slots), 1) < count_ref[0, o]
        where = slice(o * slots, (o + 1) * slots)
        column = as_column(jnp.where(live, list_ref[0, 0, o : o + 1, :] - anchor, -1).astype(F32))
        first[where, :] = (spots == column).astype(BF)
        column = as_column((list_ref[0, 1, o : o + 1, :] - anchor).astype(F32))
        own[where, :] = (spots == column).astype(BF)
        next_ref[where, :] = (spots == column - rows).astype(BF)
    marks = mark_ref[...].astype(BF)

    def body(i, at):
        a_hot, b_hot = first[at, :], own[at, :]
        source_mark_ref[at, :] = dot_across(a_hot, marks)
        own_mark_ref[at, :] = dot_across(b_hot, marks)
        zero = jnp.zeros((step, NF // 2), F32)
        store_sums(sum_ref, at, *first_terms(at, white_ref, segs, 0, a_hot, b_hot, source_ref, zero, zero))

    in_steps(step, owners * slots, body)


def given_kernel(step, early_ref, late_ref, first, own, sum_ref, source_ref, out_ref):
    rows = first.shape[1]

    def body(i, at):
        sums = load_sums(sum_ref, at)
        for ref, base in ((early_ref, 0), (late_ref, FIRST)):
            sums = first_terms(at, ref, ref.shape[0] // rows, base, first[at, :], own[at, :], source_ref, *sums)
        store_sums(out_ref, at, *sums)

    in_steps(step, sum_ref.shape[0], body)


def early_kernel(
    step, white_ref, given_ref, source_ref, other_ref, next_ref, sum_ref, source_mark_ref, own_mark_ref, out_ref, tail_ref
):
    pairs, rows = next_ref.shape
    segs = source_mark_ref.shape[1]
    per = pairs // tail_ref.shape[0]
    next_marks = white_ref[segs * rows :, :LANES].astype(F32)[:segs, :rows].astype(BF)

    def body(i, at):
        to = pl.ds(i * (step // per), step // per)
        hot = next_ref[at, :]
        sums = more_terms(at, white_ref, segs, 0, hot, source_ref, *load_sums(sum_ref, at))
        store_sums(out_ref, at, *more_terms(at, given_ref, FIRST, 0, hot, other_ref, *sums))
        both = source_mark_ref[at, :] * (own_mark_ref[at, :] + dot_across(hot, next_marks))
        shared = jnp.broadcast_to(jnp.sum(both, axis=1, keepdims=True), (step, LANES)).reshape(-1, per, LANES)
        tail = shared[:, :8, :]
        lane = lax.broadcasted_iota(jnp.int32, tail.shape, 2)
        for k in range(1, per // 8):
            tail = jnp.where(lane >= k * 8 * LANES // per, shared[:, 8 * k : 8 * k + 8, :], tail)
        tail_ref[to, :, :] = tail

    in_steps(step, pairs, body)


def late_kernel(step, given_ref, other_ref, next_ref, sum_ref, tail_ref, out_ref):
    pairs = sum_ref.shape[0]
    per = pairs // out_ref.shape[0]
    late = other_ref.shape[0] - FIRST
    out_ref[:, 2 * per :, :] = tail_ref[...].astype(BF)

    def body(i, at):
        to = pl.ds(i * (step // per), step // per)
        sums = more_terms(at, given_ref, late, FIRST, next_ref[at, :], other_ref, *load_sums(sum_ref, at))
        for k, part in enumerate(sums):
            out_ref[to, k * per : (k + 1) * per, :] = part.astype(BF).reshape(-1, per, LANES)

    in_steps(step, pairs, body)


def lags_kernel(parts, per, x_ref, high_ref, low_ref, out_hbm, held, sem):
    dests, length, _ = x_ref.shape
    total = jnp.sum(x_ref[...].astype(F32).reshape(dests // parts, parts // 2, 2, length, LANES), axis=1)
    scale = 1.0 / jnp.maximum(total[:, 0, 2 * per :, :] + total[:, 1, 2 * per :, :], 1.0)
    scale = jnp.concatenate(
        [scale[:, :, k * 8 * LANES // per :][:, :, :1] for k in range(per // 8)], axis=1
    )
    stacked = jnp.concatenate(
        [
            (total[:, k // 2, k % 2 * per : (k % 2 + 1) * per, :] * scale).reshape(-1, LANES)
            for k in range(4)
        ],
        axis=1,
    )
    coarse, fine = halves(stacked)
    both = jnp.concatenate([coarse, fine], axis=0)
    count = stacked.shape[0]
    copies = []
    for k in range(HALVES):
        columns = slice(k * NLAG // HALVES, (k + 1) * NLAG // HALVES)
        product = dot(both, high_ref[:, columns])
        traces = product[:count] + product[count:] + dot(coarse, low_ref[:, columns])
        held[:, :, columns] = traces.reshape(held.shape[0], held.shape[1], -1)
        part = pl.ds(k * NLAG // HALVES, NLAG // HALVES)
        copies.append(pltpu.make_async_copy(held.at[:, :, part], out_hbm.at[:, :, part], sem.at[k]))
        copies[-1].start()
    for copy in copies:
        copy.wait()


def call(kernel, shape, args, specs, scratch=(), mib=24, out=VMEM):
    return pl.pallas_call(
        kernel,
        out_shape=shape,
        in_specs=specs,
        out_specs=[out] * len(shape),
        scratch_shapes=list(scratch),
        compiler_params=pltpu.CompilerParams(vmem_limit_bytes=mib << 20),
    )(*args)


def local(records, gap_mask, pair_list, pair_counts):
    rows, segs, span = records.shape
    owners, slots = pair_list.shape[2:]
    chan, nbr = lax.axis_size("chan"), lax.axis_size("nbr")
    per = slots // nbr
    pairs = owners * slots
    step = min(STEP, pairs)
    back = [(i, i - 1) for i in range(1, chan)]
    swap = [(i, i ^ 1) for i in range(nbr)]
    late = segs - FIRST
    shape = jax.ShapeDtypeStruct
    tables = forward_tables(span)
    inputs = (jnp.transpose(records, (1, 0, 2)), gap_mask.T, jnp.asarray(tables), jnp.asarray(taper()))
    extra = -(-segs // 16) * 16
    keep, give_early, rest, table, window, factors, mark_rows = call(
        first_kernel,
        [
            shape((FIRST * rows, NF), BF),
            shape((FIRST * rows, NF), BF),
            shape((late, rows, span), F32),
            shape(tables.shape, BF),
            shape((1, 2 * NF), F32),
            shape((late * rows, 1), F32),
            shape((extra, NF), BF),
        ],
        [pltpu.with_memory_space_constraint(v, pltpu.HBM) for v in inputs],
        [HBM] * 4,
        [
            pltpu.VMEM((FIRST, rows, span), F32),
            pltpu.VMEM((segs, rows), jnp.int32),
            pltpu.VMEM((extra, NF), F32),
            pltpu.SemaphoreType.DMA((5,)),
        ],
        mib=32,
    )
    got_early = lax.ppermute(give_early, "nbr", swap)
    keep, give_late = call(
        second_kernel,
        [shape((segs * rows + extra, NF), BF), shape((late * rows, NF), BF)],
        (rest, table, window, factors, keep, mark_rows),
        [VMEM] * 6,
    )
    got_late = lax.ppermute(give_late, "nbr", swap)
    next_keep = lax.ppermute(keep, "chan", back)
    next_got_early = lax.ppermute(got_early, "chan", back)
    next_got_late = lax.ppermute(got_late, "chan", back)
    hots = [shape((pairs, rows), BF)] * 3
    source, sums, first, own, hot, source_marks, own_marks = call(
        functools.partial(sources_kernel, step),
        [shape((segs, pairs, NF), F32), shape((pairs, NF), F32)] + hots + [shape((pairs, segs), F32)] * 2,
        (keep, gap_mask.T, pair_list, pair_counts),
        [VMEM] * 3 + [SMEM],
        mib=32,
    )
    other, sums = call(
        functools.partial(given_kernel, step),
        [shape((segs, pairs, NF), F32), shape((pairs, NF), F32)],
        (got_early, got_late, first, own, sums),
        [VMEM] * 5,
        mib=32,
    )
    sums, tail = call(
        functools.partial(early_kernel, step),
        [shape((pairs, NF), F32), shape((chan * nbr, 8, LANES), F32)],
        (next_keep, next_got_early, source, other, hot, sums, source_marks, own_marks),
        [VMEM] * 8,
        mib=32,
    )
    (cross,) = call(
        functools.partial(late_kernel, step),
        [shape((chan * nbr, 2 * per + 8, LANES), BF)],
        (next_got_late, other, hot, sums, tail),
        [VMEM] * 5,
        mib=32,
    )
    arrived = lax.all_to_all(cross, ("chan", "nbr"), split_axis=0, concat_axis=0, tiled=True)
    high, low = inverse_tables(span)
    (traces,) = call(
        functools.partial(lags_kernel, nbr, per),
        [shape((chan, per, NLAG), F32)],
        (arrived, jnp.asarray(high), jnp.asarray(low)),
        [VMEM] * 3,
        [pltpu.VMEM((chan, per, NLAG), F32), pltpu.SemaphoreType.DMA((HALVES,))],
        out=HBM,
    )
    return traces[None]


def solution(mesh):
    return jax.shard_map(
        local,
        mesh=mesh,
        in_specs=(
            P("chan", "nbr", None),
            P("chan", "nbr"),
            P("chan", None, None, None),
            P("chan", None),
        ),
        out_specs=P("chan", None, "nbr", None),
        check_vma=False,
    )
```

```python
import functools
import math

import jax
import jax.numpy as jnp
import ml_dtypes
import numpy as np
from jax import lax
from jax.experimental import pallas as pl
from jax.experimental.pallas import tpu as pltpu
from jax.sharding import PartitionSpec as P

NF = 256
NLAG = 1024
LANES = 128
BF = jnp.bfloat16
F32 = jnp.float32
VMEM = pl.BlockSpec(memory_space=pltpu.VMEM)
HBM = pl.BlockSpec(memory_space=pltpu.HBM)
SMEM = pl.BlockSpec(memory_space=pltpu.SMEM)

EVEN, ODD = np.arange(2, NF + 1, 2), np.arange(1, NF + 1, 2)
FIRST = 4
STEP = 512
HALVES = 2


def two_parts(table):
    high = table.astype(ml_dtypes.bfloat16)
    return high, (table - high.astype(np.float64)).astype(ml_dtypes.bfloat16)


def forward_tables(span):
    clock = np.arange(span // 2)[:, None]
    parts = []
    for bins in (EVEN, ODD):
        angle = (clock * bins[None, :] % span) * (2.0 * math.pi / span)
        table = np.concatenate([np.cos(angle), -np.sin(angle)], axis=1)
        parts.append(np.concatenate(two_parts(table), axis=0))
    return np.stack(parts)


def inverse_tables(span):
    lag = np.arange(NLAG)[None, :] - NLAG // 2
    rows = []
    for bins in (EVEN, ODD):
        angle = (bins[:, None] * lag % span) * (2.0 * math.pi / span)
        rows += [np.cos(angle), -np.sin(angle)]
    return two_parts(np.concatenate(rows, axis=0))


def taper():
    window = np.sin(math.pi * np.concatenate([EVEN, EVEN, ODD, ODD]) / (NF + 1.0))
    return window[None, :].astype(np.float32)


def halves(value):
    high = value.astype(BF)
    return high, (value - high.astype(F32)).astype(BF)


def dot(a, b):
    return jnp.dot(a, b, preferred_element_type=F32)


def dot_across(a, b):
    return lax.dot_general(a, b, (((1,), (1,)), ((), ())), preferred_element_type=F32)


def as_column(row):
    size = row.shape[1]
    shape = (size, size)
    same = lax.broadcasted_iota(jnp.int32, shape, 0) == lax.broadcasted_iota(jnp.int32, shape, 1)
    return jnp.sum(jnp.where(same, row, 0.0), axis=1, keepdims=True)


def whiten(x_ref, flags, table_ref, taper_ref):
    segs, rows, span = x_ref.shape
    half = span // 2
    low = x_ref[:, :, :half].reshape(segs * rows, half)
    high = x_ref[:, :, half:].reshape(segs * rows, half)
    found = []
    for i, folded in enumerate((low + high, low - high)):
        coarse, fine = halves(folded)
        found.append(
            dot(fine, table_ref[i, :half, :]) + dot(jnp.concatenate([coarse, coarse], axis=1), table_ref[i])
        )
    even, odd = found
    energy = jnp.sum(even * even + odd * odd, axis=1, keepdims=True) * (0.5 / NF)
    factor = flags / jnp.sqrt(energy + 1e-05)
    return [
        part * factor * taper_ref[:, i * NF : (i + 1) * NF] for i, part in enumerate(found)
    ]


def share(found, keep_ref, give_ref, base):
    odd = lax.axis_index("nbr") % 2 == 1
    even_bins, odd_bins = found
    rows = even_bins.shape[0]
    keep_ref[base : base + rows, :] = jnp.where(odd, odd_bins, even_bins).astype(BF)
    give_ref[...] = jnp.where(odd, even_bins, odd_bins).astype(BF)


def first_kernel(
    x_hbm, mark_hbm, table_hbm, taper_hbm, keep_ref, give_ref, rest, table, window, factors, mark_rows, x, mark, row, sem
):
    total, rows, _ = x_hbm.shape
    early = x.shape[0]
    small = [
        pltpu.make_async_copy(mark_hbm, mark, sem.at[0]),
        pltpu.make_async_copy(taper_hbm, window, sem.at[1]),
    ]
    large = [
        pltpu.make_async_copy(table_hbm, table, sem.at[2]),
        pltpu.make_async_copy(x_hbm.at[pl.ds(0, early)], x, sem.at[3]),
        pltpu.make_async_copy(x_hbm.at[pl.ds(early, total - early)], rest, sem.at[4]),
    ]
    for copy in small + large[:2]:
        copy.start()
    for copy in small:
        copy.wait()
    large[2].start()
    flags = [as_column(mark[s : s + 1, :].astype(F32)) for s in range(total)]
    factors[...] = jnp.concatenate(flags[early:], axis=0)
    row[...] = jnp.zeros(row.shape, F32)
    row[:total, :rows] = mark[...].astype(F32)
    mark_rows[...] = row[...].astype(BF)
    large[0].wait()
    large[1].wait()
    found = whiten(x, jnp.concatenate(flags[:early], axis=0), table, window)
    share(found, keep_ref, give_ref, 0)
    large[2].wait()


def second_kernel(x_ref, table_ref, window_ref, factor_ref, early_ref, mark_rows, keep_ref, give_ref):
    found = whiten(x_ref, factor_ref[...], table_ref, window_ref)
    count = early_ref.shape[0]
    keep_ref[:count, :] = early_ref[...]
    share(found, keep_ref, give_ref, count)
    keep_ref[count + give_ref.shape[0] :, :] = mark_rows[...]


def add_products(real, imag, a, b):
    quad = NF // 2
    ar, ai, br, bi = a[:, :quad], a[:, quad:], b[:, :quad], b[:, quad:]
    return real + (ar * br + ai * bi), imag + (ai * br - ar * bi)


def first_terms(at, white_ref, segs, base, a_hot, b_hot, source_ref, real, imag):
    rows = a_hot.shape[1]
    for s in range(segs):
        white = white_ref[s * rows : (s + 1) * rows, :]
        a = dot(a_hot, white)
        source_ref[base + s, at, :] = a
        real, imag = add_products(real, imag, a, dot(b_hot, white))
    return real, imag


def more_terms(at, white_ref, segs, base, hot, source_ref, real, imag):
    rows = hot.shape[1]
    for s in range(segs):
        b = dot(hot, white_ref[s * rows : (s + 1) * rows, :])
        real, imag = add_products(real, imag, source_ref[base + s, at, :], b)
    return real, imag


def load_sums(sum_ref, at):
    return sum_ref[at, : NF // 2], sum_ref[at, NF // 2 :]


def store_sums(sum_ref, at, real, imag):
    sum_ref[at, : NF // 2] = real
    sum_ref[at, NF // 2 :] = imag


def in_steps(step, pairs, body):
    def run(i, carry):
        body(i, pl.ds(pl.multiple_of(i * step, step), step))
        return carry

    lax.fori_loop(0, pairs // step, run, 0)


def sources_kernel(
    step, white_ref, mark_ref, list_ref, count_ref,
    source_ref, sum_ref, first, own, next_ref, source_mark_ref, own_mark_ref,
):
    segs, rows = mark_ref.shape
    owners, slots = list_ref.shape[2:]
    anchor = lax.axis_index("chan") * rows
    spots = lax.broadcasted_iota(jnp.int32, (slots, rows), 1).astype(F32)
    for o in range(owners):
        live = lax.broadcasted_iota(jnp.int32, (1, slots), 1) < count_ref[0, o]
        where = slice(o * slots, (o + 1) * slots)
        column = as_column(jnp.where(live, list_ref[0, 0, o : o + 1, :] - anchor, -1).astype(F32))
        first[where, :] = (spots == column).astype(BF)
        column = as_column((list_ref[0, 1, o : o + 1, :] - anchor).astype(F32))
        own[where, :] = (spots == column).astype(BF)
        next_ref[where, :] = (spots == column - rows).astype(BF)
    marks = mark_ref[...].astype(BF)

    def body(i, at):
        a_hot, b_hot = first[at, :], own[at, :]
        source_mark_ref[at, :] = dot_across(a_hot, marks)
        own_mark_ref[at, :] = dot_across(b_hot, marks)
        zero = jnp.zeros((step, NF // 2), F32)
        store_sums(sum_ref, at, *first_terms(at, white_ref, segs, 0, a_hot, b_hot, source_ref, zero, zero))

    in_steps(step, owners * slots, body)


def given_kernel(step, early_ref, late_ref, first, own, sum_ref, source_ref, out_ref):
    rows = first.shape[1]

    def body(i, at):
        sums = load_sums(sum_ref, at)
        for ref, base in ((early_ref, 0), (late_ref, FIRST)):
            sums = first_terms(at, ref, ref.shape[0] // rows, base, first[at, :], own[at, :], source_ref, *sums)
        store_sums(out_ref, at, *sums)

    in_steps(step, sum_ref.shape[0], body)


def early_kernel(
    step, white_ref, given_ref, source_ref, other_ref, next_ref, sum_ref, source_mark_ref, own_mark_ref, out_ref, tail_ref
):
    pairs, rows = next_ref.shape
    segs = source_mark_ref.shape[1]
    per = pairs // tail_ref.shape[0]
    next_marks = white_ref[segs * rows :, :LANES].astype(F32)[:segs, :rows].astype(BF)

    def body(i, at):
        to = pl.ds(i * (step // per), step // per)
        hot = next_ref[at, :]
        sums = more_terms(at, white_ref, segs, 0, hot, source_ref, *load_sums(sum_ref, at))
        store_sums(out_ref, at, *more_terms(at, given_ref, FIRST, 0, hot, other_ref, *sums))
        both = source_mark_ref[at, :] * (own_mark_ref[at, :] + dot_across(hot, next_marks))
        shared = jnp.broadcast_to(jnp.sum(both, axis=1, keepdims=True), (step, LANES)).reshape(-1, per, LANES)
        tail = shared[:, :8, :]
        lane = lax.broadcasted_iota(jnp.int32, tail.shape, 2)
        for k in range(1, per // 8):
            tail = jnp.where(lane >= k * 8 * LANES // per, shared[:, 8 * k : 8 * k + 8, :], tail)
        tail_ref[to, :, :] = tail

    in_steps(step, pairs, body)


def late_kernel(step, given_ref, other_ref, next_ref, sum_ref, tail_ref, out_ref):
    pairs = sum_ref.shape[0]
    per = pairs // out_ref.shape[0]
    late = other_ref.shape[0] - FIRST
    out_ref[:, 2 * per :, :] = tail_ref[...].astype(BF)

    def body(i, at):
        to = pl.ds(i * (step // per), step // per)
        sums = more_terms(at, given_ref, late, FIRST, next_ref[at, :], other_ref, *load_sums(sum_ref, at))
        for k, part in enumerate(sums):
            out_ref[to, k * per : (k + 1) * per, :] = part.astype(BF).reshape(-1, per, LANES)

    in_steps(step, pairs, body)


def lags_kernel(parts, per, x_ref, high_ref, low_ref, out_hbm, held, sem):
    dests, length, _ = x_ref.shape
    total = jnp.sum(x_ref[...].astype(F32).reshape(dests // parts, parts // 2, 2, length, LANES), axis=1)
    scale = 1.0 / jnp.maximum(total[:, 0, 2 * per :, :] + total[:, 1, 2 * per :, :], 1.0)
    scale = jnp.concatenate(
        [scale[:, :, k * 8 * LANES // per :][:, :, :1] for k in range(per // 8)], axis=1
    )
    stacked = jnp.concatenate(
        [
            (total[:, k // 2, k % 2 * per : (k % 2 + 1) * per, :] * scale).reshape(-1, LANES)
            for k in range(4)
        ],
        axis=1,
    )
    coarse, fine = halves(stacked)
    both = jnp.concatenate([coarse, fine], axis=0)
    count = stacked.shape[0]
    copies = []
    for k in range(HALVES):
        columns = slice(k * NLAG // HALVES, (k + 1) * NLAG // HALVES)
        product = dot(both, high_ref[:, columns])
        traces = product[:count] + product[count:] + dot(coarse, low_ref[:, columns])
        held[:, :, columns] = traces.reshape(held.shape[0], held.shape[1], -1)
        part = pl.ds(k * NLAG // HALVES, NLAG // HALVES)
        copies.append(pltpu.make_async_copy(held.at[:, :, part], out_hbm.at[:, :, part], sem.at[k]))
        copies[-1].start()
    for copy in copies:
        copy.wait()


def call(kernel, shape, args, specs, scratch=(), mib=24, out=VMEM, us=0):
    return pl.pallas_call(
        kernel,
        out_shape=shape,
        in_specs=specs,
        out_specs=[out] * len(shape),
        scratch_shapes=list(scratch),
        compiler_params=pltpu.CompilerParams(vmem_limit_bytes=mib << 20),
        cost_estimate=pl.CostEstimate(flops=us * 10**9, bytes_accessed=us * 10**6, transcendentals=0) if us else None,
    )(*args)


def local(records, gap_mask, pair_list, pair_counts):
    rows, segs, span = records.shape
    owners, slots = pair_list.shape[2:]
    chan, nbr = lax.axis_size("chan"), lax.axis_size("nbr")
    per = slots // nbr
    pairs = owners * slots
    step = min(STEP, pairs)
    back = [(i, i - 1) for i in range(1, chan)]
    swap = [(i, i ^ 1) for i in range(nbr)]
    late = segs - FIRST
    shape = jax.ShapeDtypeStruct
    tables = forward_tables(span)
    inputs = (jnp.transpose(records, (1, 0, 2)), gap_mask.T, jnp.asarray(tables), jnp.asarray(taper()))
    extra = -(-segs // 16) * 16
    keep, give_early, rest, table, window, factors, mark_rows = call(
        first_kernel,
        [
            shape((FIRST * rows, NF), BF),
            shape((FIRST * rows, NF), BF),
            shape((late, rows, span), F32),
            shape(tables.shape, BF),
            shape((1, 2 * NF), F32),
            shape((late * rows, 1), F32),
            shape((extra, NF), BF),
        ],
        [pltpu.with_memory_space_constraint(v, pltpu.HBM) for v in inputs],
        [HBM] * 4,
        [
            pltpu.VMEM((FIRST, rows, span), F32),
            pltpu.VMEM((segs, rows), jnp.int32),
            pltpu.VMEM((extra, NF), F32),
            pltpu.SemaphoreType.DMA((5,)),
        ],
        mib=32,
    )
    got_early = lax.ppermute(give_early, "nbr", swap)
    keep, give_late = call(
        second_kernel,
        [shape((segs * rows + extra, NF), BF), shape((late * rows, NF), BF)],
        (rest, table, window, factors, keep, mark_rows),
        [VMEM] * 6,
        us=10,
    )
    got_late = lax.ppermute(give_late, "nbr", swap)
    next_keep = lax.ppermute(keep, "chan", back)
    next_got_early = lax.ppermute(got_early, "chan", back)
    cross_over = [(i * nbr + k, (i - 1) * nbr + (k ^ 1)) for i in range(1, chan) for k in range(nbr)]
    next_got_late = lax.ppermute(give_late, ("chan", "nbr"), cross_over)
    hots = [shape((pairs, rows), BF)] * 3
    source, sums, first, own, hot, source_marks, own_marks = call(
        functools.partial(sources_kernel, step),
        [shape((segs, pairs, NF), F32), shape((pairs, NF), F32)] + hots + [shape((pairs, segs), F32)] * 2,
        (keep, gap_mask.T, pair_list, pair_counts),
        [VMEM] * 3 + [SMEM],
        mib=32,
    )
    other, sums = call(
        functools.partial(given_kernel, step),
        [shape((segs, pairs, NF), F32), shape((pairs, NF), F32)],
        (got_early, got_late, first, own, sums),
        [VMEM] * 5,
        mib=32,
        us=1,
    )
    sums, tail = call(
        functools.partial(early_kernel, step),
        [shape((pairs, NF), F32), shape((chan * nbr, 8, LANES), F32)],
        (next_keep, next_got_early, source, other, hot, sums, source_marks, own_marks),
        [VMEM] * 8,
        mib=32,
    )
    (cross,) = call(
        functools.partial(late_kernel, step),
        [shape((chan * nbr, 2 * per + 8, LANES), BF)],
        (next_got_late, other, hot, sums, tail),
        [VMEM] * 5,
        mib=32,
    )
    arrived = lax.all_to_all(cross, ("chan", "nbr"), split_axis=0, concat_axis=0, tiled=True)
    high, low = inverse_tables(span)
    (traces,) = call(
        functools.partial(lags_kernel, nbr, per),
        [shape((chan, per, NLAG), F32)],
        (arrived, jnp.asarray(high), jnp.asarray(low)),
        [VMEM] * 3,
        [pltpu.VMEM((chan, per, NLAG), F32), pltpu.SemaphoreType.DMA((HALVES,))],
        out=HBM,
    )
    return traces[None]


def solution(mesh):
    return jax.shard_map(
        local,
        mesh=mesh,
        in_specs=(
            P("chan", "nbr", None),
            P("chan", "nbr"),
            P("chan", None, None, None),
            P("chan", None),
        ),
        out_specs=P("chan", None, "nbr", None),
        check_vma=False,
    )
```

```python
import functools
import math

import jax
import jax.numpy as jnp
import ml_dtypes
import numpy as np
from jax import lax
from jax.experimental import pallas as pl
from jax.experimental.pallas import tpu as pltpu
from jax.sharding import PartitionSpec as P

NF = 256
NLAG = 1024
LANES = 128
BF = jnp.bfloat16
F32 = jnp.float32
VMEM = pl.BlockSpec(memory_space=pltpu.VMEM)
HBM = pl.BlockSpec(memory_space=pltpu.HBM)
SMEM = pl.BlockSpec(memory_space=pltpu.SMEM)

EVEN, ODD = np.arange(2, NF + 1, 2), np.arange(1, NF + 1, 2)
FIRST = 4
STEP = 512
HALVES = 2


def two_parts(table):
    high = table.astype(ml_dtypes.bfloat16)
    return high, (table - high.astype(np.float64)).astype(ml_dtypes.bfloat16)


def forward_tables(span):
    clock = np.arange(span // 2)[:, None]
    parts = []
    for bins in (EVEN, ODD):
        angle = (clock * bins[None, :] % span) * (2.0 * math.pi / span)
        table = np.concatenate([np.cos(angle), -np.sin(angle)], axis=1)
        parts.append(np.concatenate(two_parts(table), axis=0))
    return np.stack(parts)


def inverse_tables(span):
    lag = np.arange(NLAG)[None, :] - NLAG // 2
    rows = []
    for bins in (EVEN, ODD):
        angle = (bins[:, None] * lag % span) * (2.0 * math.pi / span)
        rows += [np.cos(angle), -np.sin(angle)]
    return two_parts(np.concatenate(rows, axis=0))


def taper():
    window = np.sin(math.pi * np.concatenate([EVEN, EVEN, ODD, ODD]) / (NF + 1.0))
    return window[None, :].astype(np.float32)


def halves(value):
    high = value.astype(BF)
    return high, (value - high.astype(F32)).astype(BF)


def dot(a, b):
    return jnp.dot(a, b, preferred_element_type=F32)


def dot_across(a, b):
    return lax.dot_general(a, b, (((1,), (1,)), ((), ())), preferred_element_type=F32)


def as_column(row):
    size = row.shape[1]
    shape = (size, size)
    same = lax.broadcasted_iota(jnp.int32, shape, 0) == lax.broadcasted_iota(jnp.int32, shape, 1)
    return jnp.sum(jnp.where(same, row, 0.0), axis=1, keepdims=True)


def whiten(x_ref, flags, table_ref, taper_ref):
    segs, rows, span = x_ref.shape
    half = span // 2
    low = x_ref[:, :, :half].reshape(segs * rows, half)
    high = x_ref[:, :, half:].reshape(segs * rows, half)
    found = []
    for i, folded in enumerate((low + high, low - high)):
        coarse, fine = halves(folded)
        found.append(
            dot(fine, table_ref[i, :half, :]) + dot(jnp.concatenate([coarse, coarse], axis=1), table_ref[i])
        )
    even, odd = found
    energy = jnp.sum(even * even + odd * odd, axis=1, keepdims=True) * (0.5 / NF)
    factor = flags / jnp.sqrt(energy + 1e-05)
    return [
        part * factor * taper_ref[:, i * NF : (i + 1) * NF] for i, part in enumerate(found)
    ]


def share(found, keep_ref, give_ref, base):
    odd = lax.axis_index("nbr") % 2 == 1
    even_bins, odd_bins = found
    rows = even_bins.shape[0]
    keep_ref[base : base + rows, :] = jnp.where(odd, odd_bins, even_bins).astype(BF)
    give_ref[...] = jnp.where(odd, even_bins, odd_bins).astype(BF)


def first_kernel(
    x_hbm, mark_hbm, table_hbm, taper_hbm, keep_ref, give_ref, rest, table, window, factors, mark_rows, x, mark, row, sem
):
    total, rows, _ = x_hbm.shape
    early = x.shape[0]
    small = [
        pltpu.make_async_copy(mark_hbm, mark, sem.at[0]),
        pltpu.make_async_copy(taper_hbm, window, sem.at[1]),
    ]
    large = [
        pltpu.make_async_copy(table_hbm, table, sem.at[2]),
        pltpu.make_async_copy(x_hbm.at[pl.ds(0, early)], x, sem.at[3]),
        pltpu.make_async_copy(x_hbm.at[pl.ds(early, total - early)], rest, sem.at[4]),
    ]
    for copy in small + large[:2]:
        copy.start()
    for copy in small:
        copy.wait()
    large[2].start()
    flags = [as_column(mark[s : s + 1, :].astype(F32)) for s in range(total)]
    factors[...] = jnp.concatenate(flags[early:], axis=0)
    row[...] = jnp.zeros(row.shape, F32)
    row[:total, :rows] = mark[...].astype(F32)
    mark_rows[...] = row[...].astype(BF)
    large[0].wait()
    large[1].wait()
    found = whiten(x, jnp.concatenate(flags[:early], axis=0), table, window)
    share(found, keep_ref, give_ref, 0)
    large[2].wait()


def second_kernel(x_ref, table_ref, window_ref, factor_ref, early_ref, mark_rows, keep_ref, give_ref):
    found = whiten(x_ref, factor_ref[...], table_ref, window_ref)
    count = early_ref.shape[0]
    keep_ref[:count, :] = early_ref[...]
    share(found, keep_ref, give_ref, count)
    keep_ref[count + give_ref.shape[0] :, :] = mark_rows[...]


def add_products(real, imag, a, b):
    quad = NF // 2
    ar, ai, br, bi = a[:, :quad], a[:, quad:], b[:, :quad], b[:, quad:]
    return real + (ar * br + ai * bi), imag + (ai * br - ar * bi)


def first_terms(at, white_ref, segs, base, a_hot, b_hot, source_ref, real, imag):
    rows = a_hot.shape[1]
    for s in range(segs):
        white = white_ref[s * rows : (s + 1) * rows, :]
        a = dot(a_hot, white)
        source_ref[base + s, at, :] = a
        real, imag = add_products(real, imag, a, dot(b_hot, white))
    return real, imag


def more_terms(at, white_ref, segs, base, hot, source_ref, real, imag):
    rows = hot.shape[1]
    for s in range(segs):
        b = dot(hot, white_ref[s * rows : (s + 1) * rows, :])
        real, imag = add_products(real, imag, source_ref[base + s, at, :], b)
    return real, imag


def load_sums(sum_ref, at):
    return sum_ref[at, : NF // 2], sum_ref[at, NF // 2 :]


def store_sums(sum_ref, at, real, imag):
    sum_ref[at, : NF // 2] = real
    sum_ref[at, NF // 2 :] = imag


def in_steps(step, pairs, body):
    def run(i, carry):
        body(i, pl.ds(pl.multiple_of(i * step, step), step))
        return carry

    lax.fori_loop(0, pairs // step, run, 0)


def sources_kernel(
    step, white_ref, mark_ref, list_ref, count_ref,
    source_ref, sum_ref, first, own, next_ref, source_mark_ref, own_mark_ref,
):
    segs, rows = mark_ref.shape
    owners, slots = list_ref.shape[2:]
    anchor = lax.axis_index("chan") * rows
    spots = lax.broadcasted_iota(jnp.int32, (slots, rows), 1).astype(F32)
    for o in range(owners):
        live = lax.broadcasted_iota(jnp.int32, (1, slots), 1) < count_ref[0, o]
        where = slice(o * slots, (o + 1) * slots)
        column = as_column(jnp.where(live, list_ref[0, 0, o : o + 1, :] - anchor, -1).astype(F32))
        first[where, :] = (spots == column).astype(BF)
        column = as_column((list_ref[0, 1, o : o + 1, :] - anchor).astype(F32))
        own[where, :] = (spots == column).astype(BF)
        next_ref[where, :] = (spots == column - rows).astype(BF)
    marks = mark_ref[...].astype(BF)

    def body(i, at):
        a_hot, b_hot = first[at, :], own[at, :]
        source_mark_ref[at, :] = dot_across(a_hot, marks)
        own_mark_ref[at, :] = dot_across(b_hot, marks)
        zero = jnp.zeros((step, NF // 2), F32)
        store_sums(sum_ref, at, *first_terms(at, white_ref, segs, 0, a_hot, b_hot, source_ref, zero, zero))

    in_steps(step, owners * slots, body)


def given_kernel(step, early_ref, late_ref, first, own, sum_ref, source_ref, out_ref):
    rows = first.shape[1]

    def body(i, at):
        sums = load_sums(sum_ref, at)
        for ref, base in ((early_ref, 0), (late_ref, FIRST)):
            sums = first_terms(at, ref, ref.shape[0] // rows, base, first[at, :], own[at, :], source_ref, *sums)
        store_sums(out_ref, at, *sums)

    in_steps(step, sum_ref.shape[0], body)


def early_kernel(
    step, white_ref, given_ref, source_ref, other_ref, next_ref, sum_ref, source_mark_ref, own_mark_ref, out_ref, tail_ref
):
    pairs, rows = next_ref.shape
    segs = source_mark_ref.shape[1]
    per = pairs // tail_ref.shape[0]
    next_marks = white_ref[segs * rows :, :LANES].astype(F32)[:segs, :rows].astype(BF)

    def body(i, at):
        to = pl.ds(i * (step // per), step // per)
        hot = next_ref[at, :]
        sums = more_terms(at, white_ref, segs, 0, hot, source_ref, *load_sums(sum_ref, at))
        store_sums(out_ref, at, *more_terms(at, given_ref, FIRST, 0, hot, other_ref, *sums))
        both = source_mark_ref[at, :] * (own_mark_ref[at, :] + dot_across(hot, next_marks))
        shared = jnp.broadcast_to(jnp.sum(both, axis=1, keepdims=True), (step, LANES)).reshape(-1, per, LANES)
        tail = shared[:, :8, :]
        lane = lax.broadcasted_iota(jnp.int32, tail.shape, 2)
        for k in range(1, per // 8):
            tail = jnp.where(lane >= k * 8 * LANES // per, shared[:, 8 * k : 8 * k + 8, :], tail)
        tail_ref[to, :, :] = tail

    in_steps(step, pairs, body)


def late_kernel(step, given_ref, other_ref, next_ref, sum_ref, tail_ref, out_ref):
    pairs = sum_ref.shape[0]
    per = pairs // out_ref.shape[0]
    late = other_ref.shape[0] - FIRST
    out_ref[:, 2 * per :, :] = tail_ref[...].astype(BF)

    def body(i, at):
        to = pl.ds(i * (step // per), step // per)
        sums = more_terms(at, given_ref, late, FIRST, next_ref[at, :], other_ref, *load_sums(sum_ref, at))
        for k, part in enumerate(sums):
            out_ref[to, k * per : (k + 1) * per, :] = part.astype(BF).reshape(-1, per, LANES)

    in_steps(step, pairs, body)


def lags_kernel(parts, per, x_ref, high_ref, low_ref, out_hbm, held, sem):
    dests, length, _ = x_ref.shape
    total = jnp.sum(x_ref[...].astype(F32).reshape(dests // parts, parts // 2, 2, length, LANES), axis=1)
    scale = 1.0 / jnp.maximum(total[:, 0, 2 * per :, :] + total[:, 1, 2 * per :, :], 1.0)
    scale = jnp.concatenate(
        [scale[:, :, k * 8 * LANES // per :][:, :, :1] for k in range(per // 8)], axis=1
    )
    stacked = jnp.concatenate(
        [
            (total[:, k // 2, k % 2 * per : (k % 2 + 1) * per, :] * scale).reshape(-1, LANES)
            for k in range(4)
        ],
        axis=1,
    )
    coarse = stacked.astype(BF)
    copies = []
    for k in range(HALVES):
        columns = slice(k * NLAG // HALVES, (k + 1) * NLAG // HALVES)
        traces = dot(coarse, high_ref[:, columns]) + dot(coarse, low_ref[:, columns])
        held[:, :, columns] = traces.reshape(held.shape[0], held.shape[1], -1)
        part = pl.ds(k * NLAG // HALVES, NLAG // HALVES)
        copies.append(pltpu.make_async_copy(held.at[:, :, part], out_hbm.at[:, :, part], sem.at[k]))
        copies[-1].start()
    for copy in copies:
        copy.wait()


def call(kernel, shape, args, specs, scratch=(), mib=24, out=VMEM, us=0):
    return pl.pallas_call(
        kernel,
        out_shape=shape,
        in_specs=specs,
        out_specs=[out] * len(shape),
        scratch_shapes=list(scratch),
        compiler_params=pltpu.CompilerParams(vmem_limit_bytes=mib << 20),
        cost_estimate=pl.CostEstimate(flops=us * 10**9, bytes_accessed=us * 10**6, transcendentals=0) if us else None,
    )(*args)


def local(records, gap_mask, pair_list, pair_counts):
    rows, segs, span = records.shape
    owners, slots = pair_list.shape[2:]
    chan, nbr = lax.axis_size("chan"), lax.axis_size("nbr")
    per = slots // nbr
    pairs = owners * slots
    step = min(STEP, pairs)
    back = [(i, i - 1) for i in range(1, chan)]
    swap = [(i, i ^ 1) for i in range(nbr)]
    late = segs - FIRST
    shape = jax.ShapeDtypeStruct
    tables = forward_tables(span)
    inputs = (jnp.transpose(records, (1, 0, 2)), gap_mask.T, jnp.asarray(tables), jnp.asarray(taper()))
    extra = -(-segs // 16) * 16
    keep, give_early, rest, table, window, factors, mark_rows = call(
        first_kernel,
        [
            shape((FIRST * rows, NF), BF),
            shape((FIRST * rows, NF), BF),
            shape((late, rows, span), F32),
            shape(tables.shape, BF),
            shape((1, 2 * NF), F32),
            shape((late * rows, 1), F32),
            shape((extra, NF), BF),
        ],
        [pltpu.with_memory_space_constraint(v, pltpu.HBM) for v in inputs],
        [HBM] * 4,
        [
            pltpu.VMEM((FIRST, rows, span), F32),
            pltpu.VMEM((segs, rows), jnp.int32),
            pltpu.VMEM((extra, NF), F32),
            pltpu.SemaphoreType.DMA((5,)),
        ],
        mib=32,
    )
    got_early = lax.ppermute(give_early, "nbr", swap)
    keep, give_late = call(
        second_kernel,
        [shape((segs * rows + extra, NF), BF), shape((late * rows, NF), BF)],
        (rest, table, window, factors, keep, mark_rows),
        [VMEM] * 6,
        us=10,
    )
    got_late = lax.ppermute(give_late, "nbr", swap)
    next_keep = lax.ppermute(keep, "chan", back)
    next_got_early = lax.ppermute(got_early, "chan", back)
    cross_over = [(i * nbr + k, (i - 1) * nbr + (k ^ 1)) for i in range(1, chan) for k in range(nbr)]
    next_got_late = lax.ppermute(give_late, ("chan", "nbr"), cross_over)
    hots = [shape((pairs, rows), BF)] * 3
    source, sums, first, own, hot, source_marks, own_marks = call(
        functools.partial(sources_kernel, step),
        [shape((segs, pairs, NF), F32), shape((pairs, NF), F32)] + hots + [shape((pairs, segs), F32)] * 2,
        (keep, gap_mask.T, pair_list, pair_counts),
        [VMEM] * 3 + [SMEM],
        mib=32,
    )
    other, sums = call(
        functools.partial(given_kernel, step),
        [shape((segs, pairs, NF), F32), shape((pairs, NF), F32)],
        (got_early, got_late, first, own, sums),
        [VMEM] * 5,
        mib=32,
        us=1,
    )
    sums, tail = call(
        functools.partial(early_kernel, step),
        [shape((pairs, NF), F32), shape((chan * nbr, 8, LANES), F32)],
        (next_keep, next_got_early, source, other, hot, sums, source_marks, own_marks),
        [VMEM] * 8,
        mib=32,
    )
    (cross,) = call(
        functools.partial(late_kernel, step),
        [shape((chan * nbr, 2 * per + 8, LANES), BF)],
        (next_got_late, other, hot, sums, tail),
        [VMEM] * 5,
        mib=32,
    )
    arrived = lax.all_to_all(cross, ("chan", "nbr"), split_axis=0, concat_axis=0, tiled=True)
    high, low = inverse_tables(span)
    (traces,) = call(
        functools.partial(lags_kernel, nbr, per),
        [shape((chan, per, NLAG), F32)],
        (arrived, jnp.asarray(high), jnp.asarray(low)),
        [VMEM] * 3,
        [pltpu.VMEM((chan, per, NLAG), F32), pltpu.SemaphoreType.DMA((HALVES,))],
        out=HBM,
    )
    return traces[None]


def solution(mesh):
    return jax.shard_map(
        local,
        mesh=mesh,
        in_specs=(
            P("chan", "nbr", None),
            P("chan", "nbr"),
            P("chan", None, None, None),
            P("chan", None),
        ),
        out_specs=P("chan", None, "nbr", None),
        check_vma=False,
    )
```
